128 devices in a mesh: dp: 2 (over x_hi), dap: 64 (over z, y, x_lo, core).
Axes of the slice: x: 4 (x_hi: 2, x_lo: 2; x = x_hi * 2 + x_lo), y: 4, z: 4, core: 2. Of those that a mesh axis runs over, the one named last changes fastest.
Arguments:
- pair: bfloat16 [768, 384, 128], P(('dp', 'dap')), parts along dimension 0, may hold values from -6 to 6
- grad_out: bfloat16 [768, 384, 128], P(('dp', 'dap')), parts along dimension 0, may hold values from -16 to 16
- pad_mask: int32 [768], P('dp'), parts along dimension 0, may hold values 0 or 1
- chain_ids: int32 [768], P('dp'), parts along dimension 0, may hold values from 0 to 3, never falling along the last dimension, each value on 1 to 192 neighbouring positions
- chain_bias: float32 [128], replicated, may hold values from -6 to 6
- w_in: bfloat16 [128, 512], replicated, may hold values from -0.5 to 0.5
- w_gate: bfloat16 [128, 128], replicated, may hold values from -0.5 to 0.5
- w_out: bfloat16 [128, 128], replicated, may hold values from -0.5 to 0.5
Outputs:
- update: bfloat16 [768, 384, 128], P(('dp', 'dap')), parts along dimension 0
- grad_pair: bfloat16 [768, 384, 128], P(('dp', 'dap')), parts along dimension 0
- grad_w_in: float32 [256, 512], P('dp'), parts along dimension 0
- grad_w_gate: float32 [256, 128], P('dp'), parts along dimension 0
- grad_w_out: float32 [256, 128], P('dp'), parts along dimension 0
- grad_chain_bias: float32 [256], P('dp'), parts along dimension 0
The draws below stay inside these ranges and needn't reach their ends.
There are 2 independent parts, one for each index of `dp`. The reference program is written for one: setup_inputs(seed, part) draws one part's arguments, and reference() takes and returns one part's arrays. A program takes and returns all parts, laid end to end along the dimension named above; an argument that names none is the same for every part. Nothing has to cross between parts.
Inputs may be any that keep to these rules, and one draw needn't show every extreme that they name: `chain_ids`: chain numbers never fall along the residues.
All inputs are finite; a program needn't handle non-finite values.
Results may differ from the reference program's by a relative error of at most 0.0081.
Values may be sent and summed in bfloat16 or wider, within the bound.
A program may use at most 384 MiB of HBM per device.

```python
import math
import jax
import jax.numpy as jnp
import numpy as np
from jax import lax

C = 128
CH = 128
N = 384


def set_ends(drawn, own_key, least, high):
    index_at = [jax.random.randint(jax.random.fold_in(own_key, axis), (), 0, length) for axis, length in enumerate(drawn.shape)]
    main_axis = drawn.shape.index(max(drawn.shape))
    beside = index_at[:main_axis] + [(index_at[main_axis] + 1) % drawn.shape[main_axis]] + index_at[main_axis + 1:]
    return drawn.at[tuple(index_at)].set(least).at[tuple(beside)].set(high)


def with_spikes(array, stream_key, source, target, parts, factor):
    def block_of(dim):
        return (jnp.arange(array.shape[dim]) // (array.shape[dim] // parts)).reshape((-1,) + (1,) * (array.ndim - 1 - dim))

    one_side = jax.random.permutation(stream_key, parts)[block_of(target)]
    second = (block_of(target) + parts // 2) % parts
    return jnp.where((block_of(source) == one_side) | (block_of(source) == second), factor * array, array)


def block_scale(rng, dims, shards, least, largest):
    def one(position, parts):
        draws = jax.random.uniform(jax.random.fold_in(jax.random.fold_in(rng, 6), position), (parts,), jnp.float32, least / len(shards), largest / len(shards))
        return jnp.repeat(jnp.exp(draws), dims[position] // parts).reshape((-1,) + (1,) * (len(dims) - position - 1))

    gain = one(*shards[0])
    for cut in shards[1:]:
        gain = gain * one(*cut)
    return gain


def length_profile(number_of, total, bound, lean):
    weights = [(1 << 20) // math.isqrt(grade ** lean) + 1 for grade in range(2, number_of + 1)]
    surplus, counts = total - bound - (number_of - 1), [1] * (number_of - 1)
    while surplus > 0:
        movable = [i for i in range(number_of - 1) if counts[i] < bound]
        pool, budget = sum([weights[i] for i in movable]), surplus
        for i in movable:
            addition = min(bound - counts[i], max(1, budget * weights[i] // pool), surplus)
            counts[i] = counts[i] + addition
            surplus = surplus - addition
    return np.array([bound] + counts)


def uneven(key, count, total, limit, lean):
    if count == 2:
        one = jax.random.randint(key, (), max(1, total - limit), min(limit, total - 1) + 1)
        return jnp.stack([one, total - one])
    lengths = jnp.asarray(length_profile(count, total, limit, lean), jnp.int32)
    pairs = (count - 1) // 2
    giver, sink = lengths[1:1 + 2 * pairs:2], lengths[2:2 + 2 * pairs:2]
    room = jnp.minimum(giver - 1, limit - sink)
    shifted = jax.random.randint(jax.random.fold_in(key, 1), (pairs,), 0, 1 << 20) % (room + 1)
    lengths = lengths.at[1:1 + 2 * pairs:2].set(giver - shifted).at[2:2 + 2 * pairs:2].set(sink + shifted)
    return lengths[jax.random.permutation(jax.random.fold_in(key, 2), count)]


def centred(rng, dims, spread, reach, shards=(), kind=jnp.bfloat16):
    entries = jax.random.normal(rng, dims, jnp.float32) * spread
    if len(shards) > 0:
        entries = block_scale(rng, dims, shards, -0.22, 0.18) * entries
    return jnp.clip(entries, min=-reach, max=reach).astype(kind)


def bell_draw_with(key, extent, spread, most, shards, heavy, kind=jnp.bfloat16):
    drawn = spread * jax.random.normal(key, extent, jnp.float32)
    if shards:
        drawn = drawn * block_scale(key, extent, shards, -0.22, 0.18)
    return jnp.clip(with_spikes(drawn, jax.random.fold_in(key, 3), *heavy), -most, most).astype(kind)


def setup_inputs(seed: int = 0, part: int = 0) -> dict:
    seeds = jax.random.split(jax.random.key(seed), 9)
    part_keys = jax.random.split(jax.random.fold_in(seeds[8], part), 9)
    pair = centred(part_keys[0], (N, N, C), 1.0, 6.0, ((0, 64),))
    grad_out = bell_draw_with(part_keys[1], (N, N, C), 1.0, 16.0, ((0, 64),), (0, 1, 64, 4.0))
    pad_mask = set_ends((jax.random.randint(part_keys[2], (N,), 0, 4) < 3).astype(jnp.int32), jax.random.fold_in(part_keys[2], 1), 0, 1)
    chain_ids = jnp.searchsorted(jnp.cumsum(uneven(part_keys[3], 4, N, N // 2, 2)), jnp.arange(N), side="right").astype(jnp.int32)
    chain_bias = centred(seeds[4], (C,), 1.0, 6.0, (), jnp.float32)
    w_in = centred(seeds[5], (C, 4 * CH), C ** -0.5, 0.5)
    w_gate = centred(seeds[6], (C, C), C ** -0.5, 0.5)
    w_out = centred(seeds[7], (CH, C), CH ** -0.5, 0.5)
    return dict(pair=pair, grad_out=grad_out, pad_mask=pad_mask, chain_ids=chain_ids, chain_bias=chain_bias, w_in=w_in, w_gate=w_gate, w_out=w_out)


epsilon = 1e-05

def normalize(values):
    center = values - lax.optimization_barrier(jnp.mean(values, axis=-1, keepdims=True))
    inverse = lax.rsqrt(lax.optimization_barrier(jnp.mean(center * center, axis=-1, keepdims=True)) + epsilon)
    return (center * inverse, inverse)

def norm_back(grad_norm, normed, inverse):
    first = lax.optimization_barrier(jnp.mean(grad_norm, axis=-1, keepdims=True))
    second = lax.optimization_barrier(jnp.mean(grad_norm * normed, axis=-1, keepdims=True))
    return inverse * (grad_norm - first - normed * second)

def reference(pair, grad_out, pad_mask, chain_ids, chain_bias, w_in, w_gate, w_out):
    highest = lax.Precision.HIGHEST
    same_chain = (chain_ids[:, None] == chain_ids[None, :]).astype(jnp.float32)[:, :, None]
    pad_float = pad_mask.astype(jnp.float32)
    pair_mask = (pad_float[:, None] * pad_float[None, :])[:, :, None]
    z_input = pair.astype(jnp.float32) + same_chain * chain_bias
    z_hat, z_inverse = normalize(z_input)
    z_norm = z_hat.astype(jnp.bfloat16)
    z_flat = z_norm.reshape(N * N, C)
    projected = jnp.dot(z_flat, w_in, preferred_element_type=jnp.float32).reshape(N, N, 4 * CH)
    gate_a = projected[:, :, :CH]
    proj_a = projected[:, :, CH:2 * CH]
    gate_b = projected[:, :, 2 * CH:3 * CH]
    proj_b = projected[:, :, 3 * CH:]
    sig_a = jax.nn.sigmoid(gate_a)
    sig_b = jax.nn.sigmoid(gate_b)
    left_a = (sig_a * proj_a * pair_mask).astype(jnp.bfloat16)
    right_b = (sig_b * proj_b * pair_mask).astype(jnp.bfloat16)
    mixed = jnp.einsum('ikc,jkc->ijc', left_a.astype(jnp.float32), right_b.astype(jnp.float32), precision=highest)
    x_hat, x_inverse = normalize(mixed)
    x_norm = x_hat.astype(jnp.bfloat16)
    x_flat = x_norm.reshape(N * N, CH)
    gate_logit = jnp.dot(z_flat, w_gate, preferred_element_type=jnp.float32)
    gate_value = jax.nn.sigmoid(gate_logit)
    out_lin = jnp.dot(x_flat, w_out, preferred_element_type=jnp.float32)
    update = (gate_value * out_lin).astype(jnp.bfloat16).reshape(N, N, C)
    cotangent = grad_out.astype(jnp.float32).reshape(N * N, C)
    grad_u = (cotangent * gate_value).astype(jnp.bfloat16)
    grad_s = (cotangent * out_lin * gate_value * (1.0 - gate_value)).astype(jnp.bfloat16)
    grad_w_out = jnp.dot(x_flat.T, grad_u, preferred_element_type=jnp.float32) / N
    grad_w_gate = jnp.dot(z_flat.T, grad_s, preferred_element_type=jnp.float32) / N
    grad_xn = jnp.dot(grad_u, w_out.T, preferred_element_type=jnp.float32).reshape(N, N, CH)
    grad_mixed = norm_back(grad_xn, x_hat, x_inverse).astype(jnp.bfloat16)
    grad_left = jnp.einsum('ijc,jkc->ikc', grad_mixed.astype(jnp.float32), right_b.astype(jnp.float32), precision=highest)
    grad_right = jnp.einsum('ijc,ikc->jkc', grad_mixed.astype(jnp.float32), left_a.astype(jnp.float32), precision=highest)
    grad_proj = jnp.concatenate([grad_left * proj_a * pair_mask * sig_a * (1.0 - sig_a), grad_left * sig_a * pair_mask, grad_right * proj_b * pair_mask * sig_b * (1.0 - sig_b), grad_right * sig_b * pair_mask], axis=-1).astype(jnp.bfloat16).reshape(N * N, 4 * CH)
    grad_w_in = jnp.dot(z_flat.T, grad_proj, preferred_element_type=jnp.float32) / N
    grad_zn = jnp.dot(grad_proj, w_in.T, preferred_element_type=jnp.float32)
    grad_zn = grad_zn + jnp.dot(grad_s, w_gate.T, preferred_element_type=jnp.float32)
    grad_input = norm_back(grad_zn.reshape(N, N, C), z_hat, z_inverse)
    grad_chain_bias = lax.optimization_barrier(jnp.sum(same_chain * grad_input, axis=(0, 1))) / N
    grad_pair = grad_input.astype(jnp.bfloat16)
    return (update, grad_pair, grad_w_in, grad_w_gate, grad_w_out, grad_chain_bias)
```

```python
import functools

import jax
import jax.numpy as jnp
from jax import lax
from jax.experimental import pallas as pl
from jax.experimental.pallas import tpu as pltpu
from jax.sharding import PartitionSpec as P

epsilon = 1e-05
f32 = jnp.float32
bf16 = jnp.bfloat16

RING = 4
PAIR = 2
B, A, X, DX, DA, DB = range(6)


def nn(left, right):
    return jnp.dot(left, right, preferred_element_type=f32)


def nt(left, right):
    return lax.dot_general(left, right, (((1,), (1,)), ((), ())), preferred_element_type=f32)


def sigmoid(values):
    return 0.5 * jnp.tanh(0.5 * values) + 0.5


def mean0(values):
    return jnp.mean(values, axis=0, keepdims=True)


def kernel(
    planes,
    pair, gout, pad_v, chain_v, pad_s, chain_s, bias, w_in, w_gate, w_out,
    update, gpair, gw_in, gw_gate, gw_out, gw_chain,
    s_snd, s_rcv, r_snd, r_rcv,
    z, rz, sig_a, lin_a, sig_b, lin_b, gate, gout_t, du, dxn, xn, ds,
    bias_t, wt_in, wt_gate, wt_out, gather, scatter, order, order_t, bn, dxt,
    g_sum, g_rcv, h_snd, h_rcv, o_snd, o_rcv, chain_sum,
    s_ssem, s_rsem, r_ssem, r_rsem, g_ssem, g_rsem,
):
    rows, n, channels = pair.shape
    chunks = rows // PAIR
    lanes = n // chunks
    per_plane = channels // planes
    mine = per_plane // RING
    part = planes * PAIR
    me = lax.axis_index("dap")
    plane = lax.div(me, RING)
    place = lax.rem(me, RING)

    def at_plane(k):
        return lax.rem(plane + k, planes)

    def at_place(k):
        return lax.rem(place + k, RING)

    barrier = pltpu.get_barrier_semaphore()

    @pl.loop(1, planes)
    def _(k):
        pl.semaphore_signal(barrier, inc=1, device_id={"dap": at_plane(k) * RING + place}, device_id_type=pl.DeviceIdType.MESH)

    @pl.loop(1, RING)
    def _(k):
        pl.semaphore_signal(barrier, inc=1, device_id={"dap": plane * RING + at_place(k)}, device_id_type=pl.DeviceIdType.MESH)

    def send_planes(src, dst, ssem, rsem):
        @pl.loop(1, planes)
        def _(k):
            to = at_plane(k)
            pltpu.make_async_remote_copy(
                src_ref=src(to), dst_ref=dst(plane), send_sem=ssem, recv_sem=rsem,
                device_id={"dap": to * RING + place}, device_id_type=pl.DeviceIdType.MESH,
            ).start()

    def send_places(src, dst, ssem, rsem):
        @pl.loop(1, RING)
        def _(k):
            to = at_place(k)
            pltpu.make_async_remote_copy(
                src_ref=src(to), dst_ref=dst(place), send_sem=ssem, recv_sem=rsem,
                device_id={"dap": plane * RING + to}, device_id_type=pl.DeviceIdType.MESH,
            ).start()

    def wait(ref, sem):
        pltpu.make_async_copy(ref, ref, sem).wait()

    def s_send(u, p):
        send_planes(lambda to: s_snd.at[u, p, to], lambda own: s_rcv.at[u, p, own], s_ssem.at[u, p], s_rsem.at[u, p])
        s_rcv[u, p, plane] = s_snd[u, p, plane]

    def s_wait(u, p):
        wait(s_rcv.at[u, p, pl.ds(0, planes - 1)], s_rsem.at[u, p])

    def r_send(u, p):
        send_places(lambda to: r_snd.at[u, p, to], lambda own: r_rcv.at[u, p, own], r_ssem.at[u, p], r_rsem.at[u, p])
        r_rcv[u, p, place] = r_snd[u, p, place]

    def r_wait(u, p):
        wait(r_rcv.at[u, p, pl.ds(0, RING - 1)], r_rsem.at[u, p])

    def to_channels(u, p):
        s_wait(u, p)
        got = nn(gather[...], s_rcv[u, p].reshape(part * per_plane, n))
        r_snd[u, p] = got.astype(bf16).reshape(RING, mine, part, n)
        r_send(u, p)

    def to_rows(u, p):
        r_wait(u, p)
        got = nn(scatter[...], r_rcv[u, p].reshape(part * per_plane, n))
        s_snd[u, p] = got.astype(bf16).reshape(planes, PAIR * per_plane, n)
        s_send(u, p)

    def span(kt):
        return pl.ds(pl.multiple_of(kt * lanes, lanes), lanes)

    def put(u, p, kt, block):
        pieces = [block[:, h * lanes:(h + 1) * lanes].reshape(planes, per_plane, lanes) for h in range(PAIR)]
        s_snd[u, p, :, :, span(kt)] = jnp.concatenate(pieces, axis=1).astype(bf16)

    def take(u, p, kt):
        block = s_rcv[u, p, :, :, span(kt)].astype(f32)
        pieces = [block[:, h * per_plane:(h + 1) * per_plane, :].reshape(channels, lanes) for h in range(PAIR)]
        return jnp.concatenate(pieces, axis=1)

    def turned(ref, p, kt):
        return jnp.concatenate([ref[p * PAIR + h, span(kt), :].astype(f32).T for h in range(PAIR)], axis=1)

    def turn_back(ref, p, kt, block):
        for h in range(PAIR):
            ref[p * PAIR + h, span(kt), :] = block[:, h * lanes:(h + 1) * lanes].T.astype(bf16)

    def same_of(p, kt):
        ids = chain_v[:, span(kt)]
        return jnp.concatenate([(ids == chain_s[me * rows + p * PAIR + h]).astype(f32) for h in range(PAIR)], axis=1)

    def mask_of(p, kt):
        pad = pad_v[:, span(kt)]
        return jnp.concatenate([(pad * pad_s[me * rows + p * PAIR + h]).astype(f32) for h in range(PAIR)], axis=1)

    def project(u, p, kt, sig_ref, lin_ref, first):
        blk = p * chunks + kt
        both = nn(wt_in[first:first + 2 * channels, :], z[blk])
        sig, lin = sigmoid(both[:channels]), both[channels:]
        sig_ref[blk] = sig
        lin_ref[blk] = lin
        put(u, p, kt, sig * lin * mask_of(p, kt))

    for first in range(0, 4 * channels, channels):
        wt_in[first:first + channels, :] = w_in[:, first:first + channels].astype(f32).T.astype(bf16)
    wt_gate[...] = w_gate[...].astype(f32).T.astype(bf16)
    wt_out[...] = w_out[...].astype(f32).T.astype(bf16)
    bias_t[...] = jnp.broadcast_to(bias[...], (channels, channels)).T

    def start_block(p, kt):
        blk = p * chunks + kt
        col = bias_t[:, 0:1]
        values = turned(pair, p, kt) + same_of(p, kt) * col
        center = values - mean0(values)
        inverse = lax.rsqrt(mean0(center * center) + epsilon)
        z[blk] = (center * inverse).astype(bf16)
        rz[blk] = inverse
        project(B, p, kt, sig_b, lin_b, 2 * channels)

    @pl.loop(0, chunks)
    def _(kt):
        start_block(0, kt)

    pl.semaphore_wait(barrier, planes - 1 + RING - 1)
    s_send(B, 0)

    @pl.loop(1, chunks)
    def _(p):
        @pl.loop(0, chunks)
        def _(kt):
            start_block(p, kt)

        s_send(B, p)

    size = part * per_plane
    i0 = lax.broadcasted_iota(jnp.int32, (size, size), 0)
    i1 = lax.broadcasted_iota(jnp.int32, (size, size), 1)

    def at_owner(i):
        return lax.rem(i, part) * per_plane + lax.div(i, part)

    gather[...] = (i1 == at_owner(i0)).astype(f32).astype(bf16)
    scatter[...] = (i0 == at_owner(i1)).astype(f32).astype(bf16)
    j0 = lax.broadcasted_iota(jnp.int32, (n, n), 0)
    j1 = lax.broadcasted_iota(jnp.int32, (n, n), 1)

    def natural(i):
        row, own = lax.rem(i, PAIR), lax.rem(lax.div(i, PAIR), planes)
        at, p = lax.rem(lax.div(i, part), RING), lax.div(i, part * RING)
        return (own * RING + at) * rows + p * PAIR + row

    order[...] = (j0 == natural(j1)).astype(f32).astype(bf16)
    order_t[...] = (j1 == natural(j0)).astype(f32).astype(bf16)

    @pl.loop(0, chunks)
    def _(p):
        @pl.loop(0, chunks)
        def _(kt):
            project(A, p, kt, sig_a, lin_a, 0)

        s_send(A, p)
        to_channels(B, p)

    @pl.loop(0, chunks)
    def _(p):
        @pl.loop(0, chunks)
        def _(kt):
            blk = p * chunks + kt
            g = sigmoid(nn(wt_gate[...], z[blk]))
            cot = turned(gout, p, kt)
            gate[blk] = g
            gout_t[blk] = cot
            grad_u = (cot * g).astype(bf16)
            du[blk] = grad_u
            dxn[blk] = nn(w_out[...], grad_u)

        to_channels(A, p)

    @pl.loop(0, chunks)
    def _(p):
        r_wait(B, p)

    @pl.loop(0, mine)
    def _(c):
        rows_b = jnp.concatenate([r_rcv[B, p, :, c].reshape(RING * part, n) for p in range(chunks)], axis=0)
        bn[c] = nn(order[...], rows_b).astype(bf16)

    @pl.loop(0, chunks)
    def _(p):
        r_wait(A, p)

        @pl.loop(0, mine)
        def _(c):
            got = nt(r_rcv[A, p, :, c].reshape(RING * part, n), bn[c])
            r_snd[X, p, :, c] = got.astype(bf16).reshape(RING, part, n)

        r_send(X, p)

    @pl.loop(0, chunks)
    def _(p):
        to_rows(X, p)

    @pl.loop(0, chunks)
    def _(p):
        s_wait(X, p)

        @pl.loop(0, chunks)
        def _(kt):
            blk = p * chunks + kt
            values = take(X, p, kt)
            center = values - mean0(values)
            inverse = lax.rsqrt(mean0(center * center) + epsilon)
            normed = center * inverse
            xn[blk] = normed.astype(bf16)
            grad = dxn[blk]
            grad = inverse * (grad - mean0(grad) - normed * mean0(grad * normed))
            put(DX, p, kt, grad)

        s_send(DX, p)

    g_sum[...] = jnp.zeros_like(g_sum)
    chain_sum[...] = jnp.zeros_like(chain_sum)

    def add_sum(first, value):
        width = value.shape[1]
        g_sum[:, :, first:first + width] += value.reshape(planes, per_plane, width)

    @pl.loop(0, chunks)
    def _(p):
        @pl.loop(0, chunks)
        def _(kt):
            blk = p * chunks + kt
            lin = nn(wt_out[...], xn[blk])
            g = gate[blk]
            turn_back(update, p, kt, g * lin)
            grad_s = (gout_t[blk] * lin * g * (1.0 - g)).astype(bf16)
            ds[blk] = grad_s
            add_sum(4 * channels, nt(z[blk], grad_s))
            add_sum(5 * channels, nt(xn[blk], du[blk]))

        to_channels(DX, p)

    @pl.loop(0, chunks)
    def _(p):
        r_wait(DX, p)

        @pl.loop(0, mine)
        def _(c):
            grad = r_rcv[DX, p, :, c].reshape(RING * part, n)
            r_snd[DA, p, :, c] = nn(grad, bn[c]).astype(bf16).reshape(RING, part, n)
            dxt[c, p] = nt(order_t[...], grad).astype(bf16)

        r_send(DA, p)

    @pl.loop(0, mine)
    def _(c):
        total = nn(dxt[c, 0], r_rcv[A, 0, :, c].reshape(RING * part, n))
        for p in range(1, chunks):
            total = total + nn(dxt[c, p], r_rcv[A, p, :, c].reshape(RING * part, n))
        for p in range(chunks):
            r_snd[DB, p, :, c] = total[p * RING * part:(p + 1) * RING * part].astype(bf16).reshape(RING, part, n)

    @pl.loop(0, chunks)
    def _(p):
        r_send(DB, p)

    @pl.loop(0, chunks)
    def _(p):
        to_rows(DA, p)

    @pl.loop(0, chunks)
    def _(p):
        to_rows(DB, p)

    @pl.loop(0, chunks)
    def _(p):
        s_wait(DA, p)
        s_wait(DB, p)

        @pl.loop(0, chunks)
        def _(kt):
            blk = p * chunks + kt
            mask = mask_of(p, kt)
            parts = []
            for u, sig_ref, lin_ref in ((DA, sig_a, lin_a), (DB, sig_b, lin_b)):
                sig = sig_ref[blk]
                grad = take(u, p, kt) * mask * sig
                parts.append((grad * lin_ref[blk] * (1.0 - sig)).astype(bf16))
                parts.append(grad.astype(bf16))
            grad_proj = jnp.concatenate(parts, axis=0)
            normed = z[blk]
            add_sum(0, nt(normed, grad_proj))
            grad = nn(w_in[...], grad_proj) + nn(w_gate[...], ds[blk])
            normed = normed.astype(f32)
            grad = rz[blk] * (grad - mean0(grad) - normed * mean0(grad * normed))
            turn_back(gpair, p, kt, grad)
            chain_sum[...] += grad * same_of(p, kt)

    total = jnp.sum(chain_sum[...], axis=1, keepdims=True)
    add_sum(6 * channels, jnp.broadcast_to(total, (channels, channels)))

    send_planes(lambda to: g_sum.at[to], lambda own: g_rcv.at[own], g_ssem.at[0], g_rsem.at[0])
    g_rcv[plane] = g_sum[plane]
    wait(g_rcv.at[pl.ds(0, planes - 1)], g_rsem.at[0])
    h_snd[...] = jnp.sum(g_rcv[...], axis=0)
    send_places(lambda to: h_snd, lambda own: h_rcv.at[own], g_ssem.at[1], g_rsem.at[1])
    h_rcv[place] = h_snd[...]
    wait(h_rcv.at[pl.ds(0, RING - 1)], g_rsem.at[1])
    o_snd[...] = jnp.sum(h_rcv[...], axis=0) * (1.0 / n)
    send_planes(lambda to: o_snd, lambda own: o_rcv.at[own], g_ssem.at[2], g_rsem.at[2])
    o_rcv[plane] = o_snd[...]
    wait(o_rcv.at[pl.ds(0, planes - 1)], g_rsem.at[2])
    gw_in[...] = o_rcv[:, :, 0:4 * channels].reshape(channels, 4 * channels)
    gw_gate[...] = o_rcv[:, :, 4 * channels:5 * channels].reshape(channels, channels)
    gw_out[...] = o_rcv[:, :, 5 * channels:6 * channels].reshape(channels, channels)
    gw_chain[...] = o_rcv[:, :, 6 * channels:7 * channels].reshape(channels, channels).T[0:1, :]

    @pl.loop(0, 6)
    def _(u):
        @pl.loop(0, chunks)
        def _(p):
            wait(s_snd.at[u, p, pl.ds(0, planes - 1)], s_ssem.at[u, p])
            wait(r_snd.at[u, p, pl.ds(0, RING - 1)], r_ssem.at[u, p])

    wait(g_sum.at[pl.ds(0, planes - 1)], g_ssem.at[0])
    wait(h_rcv.at[pl.ds(0, RING - 1)], g_ssem.at[1])
    wait(o_rcv.at[pl.ds(0, planes - 1)], g_ssem.at[2])


def on_device(devices, pair, grad_out, pad_mask, chain_ids, chain_bias, w_in, w_gate, w_out):
    rows, n, channels = pair.shape
    planes = devices // RING
    chunks = rows // PAIR
    lanes = n // chunks
    per_plane = channels // planes
    mine = per_plane // RING
    part = planes * PAIR
    blocks = chunks * chunks
    wide = PAIR * lanes
    vmem, sems = pltpu.VMEM, pltpu.SemaphoreType.DMA
    scratch = [
        vmem((6, chunks, planes, PAIR * per_plane, n), bf16),
        vmem((6, chunks, planes, PAIR * per_plane, n), bf16),
        vmem((6, chunks, RING, mine, part, n), bf16),
        vmem((6, chunks, RING, mine, part, n), bf16),
        vmem((blocks, channels, wide), bf16),
        vmem((blocks, 1, wide), f32),
        vmem((blocks, channels, wide), f32),
        vmem((blocks, channels, wide), f32),
        vmem((blocks, channels, wide), f32),
        vmem((blocks, channels, wide), f32),
        vmem((blocks, channels, wide), f32),
        vmem((blocks, channels, wide), f32),
        vmem((blocks, channels, wide), bf16),
        vmem((blocks, channels, wide), f32),
        vmem((blocks, channels, wide), bf16),
        vmem((blocks, channels, wide), bf16),
        vmem((channels, channels), f32),
        vmem((4 * channels, channels), bf16),
        vmem((channels, channels), bf16),
        vmem((channels, channels), bf16),
        vmem((part * per_plane, part * per_plane), bf16),
        vmem((part * per_plane, part * per_plane), bf16),
        vmem((n, n), bf16),
        vmem((n, n), bf16),
        vmem((mine, n, n), bf16),
        vmem((mine, chunks, n, RING * part), bf16),
        vmem((planes, per_plane, 7 * channels), f32),
        vmem((planes, per_plane, 7 * channels), f32),
        vmem((per_plane, 7 * channels), f32),
        vmem((RING, per_plane, 7 * channels), f32),
        vmem((per_plane, 7 * channels), f32),
        vmem((planes, per_plane, 7 * channels), f32),
        vmem((channels, wide), f32),
        sems((6, chunks)), sems((6, chunks)), sems((6, chunks)), sems((6, chunks)), sems((3,)), sems((3,)),
    ]
    in_vmem = pl.BlockSpec(memory_space=pltpu.VMEM)
    in_smem = pl.BlockSpec(memory_space=pltpu.SMEM)
    shape = jax.ShapeDtypeStruct
    out = pl.pallas_call(
        functools.partial(kernel, planes),
        out_shape=(
            shape(pair.shape, bf16),
            shape(pair.shape, bf16),
            shape(w_in.shape, f32),
            shape(w_gate.shape, f32),
            shape(w_out.shape, f32),
            shape((1, channels), f32),
        ),
        in_specs=[in_vmem] * 4 + [in_smem] * 2 + [in_vmem] * 4,
        out_specs=[in_vmem] * 6,
        scratch_shapes=scratch,
        compiler_params=pltpu.CompilerParams(collective_id=0, has_side_effects=True, vmem_limit_bytes=56 * 2**20),
        cost_estimate=pl.CostEstimate(flops=2 * 10**9, bytes_accessed=3 * 10**6, transcendentals=10**6),
    )(
        pair, grad_out, pad_mask.reshape(1, n), chain_ids.reshape(1, n), pad_mask, chain_ids,
        chain_bias.reshape(1, channels), w_in, w_gate, w_out,
    )
    return (*out[:5], out[5].reshape(channels))


def solution(mesh):
    placed = (P(("dp", "dap"), None, None), P(("dp", "dap"), None, None), P("dp"), P("dp"), P(), P(), P(), P())
    return jax.shard_map(
        functools.partial(on_device, mesh.shape["dap"]),
        mesh=mesh,
        in_specs=placed,
        out_specs=(
            P(("dp", "dap"), None, None),
            P(("dp", "dap"), None, None),
            P("dp", None),
            P("dp", None),
            P("dp", None),
            P("dp"),
        ),
        check_vma=False,
    )
```

```python
import functools

import jax
import jax.numpy as jnp
from jax import lax
from jax.experimental import pallas as pl
from jax.experimental.pallas import tpu as pltpu
from jax.sharding import PartitionSpec as P

epsilon = 1e-05
f32 = jnp.float32
bf16 = jnp.bfloat16

CORES = 2
QUAD = 4
PAIR = 2
B, A, X, DX, DA, DB = range(6)


def nn(left, right):
    return jnp.dot(left, right, preferred_element_type=f32)


def nt(left, right):
    return lax.dot_general(left, right, (((1,), (1,)), ((), ())), preferred_element_type=f32)


def tn(left, right):
    return lax.dot_general(left, right, (((0,), (0,)), ((), ())), preferred_element_type=f32)


def sigmoid(values):
    return 0.5 * jnp.tanh(0.5 * values) + 0.5


def mean0(values):
    return jnp.mean(values, axis=0, keepdims=True)


def kernel(
    devices,
    pair, gout, pad_v, chain_v, pad_s, chain_s, bias, w_in, w_gate, w_out,
    update_t, gpair_t, sums,
    s_snd, s_rcv, b_all, ch_a, ch_dx, ch_dxo, db_part, db_snd, db_rcv, ch_db,
    z, rz, sig_a, lin_a, sig_b, lin_b, gate, gout_t, du, acc, xn, ds,
    bias_t, wt_in, wt_gate, wt_out, gather, scatter, order, bn,
    g_sum, g_rcv, h_snd, h_rcv, o_snd, chain_sum,
    s_ssem, s_rsem, b_ssem, b_rsem, d_ssem, d_rsem, g_ssem, g_rsem,
):
    rows, n, channels = pair.shape
    planes = devices // CORES
    quads = devices // QUAD
    chunks = rows // PAIR
    lanes = n // chunks
    mine = channels // planes
    part = planes * PAIR
    size = part * mine
    me = lax.axis_index("dap")
    plane = lax.div(me, CORES)
    core = lax.rem(me, CORES)
    other = plane * CORES + 1 - core
    quad = lax.div(me, QUAD)
    corner = lax.rem(me, QUAD)

    def plane_peer(k):
        to = lax.rem(plane + k, planes)
        return to, to * CORES + core

    def quad_peer(k):
        to = lax.rem(quad + k, quads)
        return to, to * QUAD + corner

    def corner_peer(k):
        to = lax.rem(corner + k, QUAD)
        return to, quad * QUAD + to

    barrier = pltpu.get_barrier_semaphore()
    pair_core = lax.rem(corner + 1, 2)
    greeted = [plane_peer(k)[1] for k in range(1, planes)] + [quad * QUAD + pair_core, quad * QUAD + pair_core + 2]
    for device in greeted:
        pl.semaphore_signal(barrier, inc=1, device_id={"dap": device}, device_id_type=pl.DeviceIdType.MESH)

    def remote(src, dst, ssem, rsem, device):
        pltpu.make_async_remote_copy(
            src_ref=src, dst_ref=dst, send_sem=ssem, recv_sem=rsem,
            device_id={"dap": device}, device_id_type=pl.DeviceIdType.MESH,
        ).start()

    def wait(ref, sem):
        pltpu.make_async_copy(ref, ref, sem).wait()

    def s_send(u, p):
        for k in range(1, planes):
            to, device = plane_peer(k)
            remote(s_snd.at[u, p, to], s_rcv.at[u, p, plane], s_ssem.at[u, p], s_rsem.at[u, p], device)
        s_rcv[u, p, plane] = s_snd[u, p, plane]

    def s_wait(u, p):
        wait(s_rcv.at[u, p, pl.ds(0, planes - 1)], s_rsem.at[u, p])

    def to_channels(u, p):
        s_wait(u, p)
        return nn(gather[...], s_rcv[u, p].reshape(size, n)).astype(bf16)

    def to_rows(u, p, values):
        s_snd[u, p] = nn(scatter[...], values).astype(bf16).reshape(planes, PAIR * mine, n)
        s_send(u, p)

    def span(kt):
        return pl.ds(pl.multiple_of(kt * lanes, lanes), lanes)

    groups = channels // 8
    low = lax.broadcasted_iota(jnp.int32, (groups, 8, lanes), 1) < 4

    def swap(first, second):
        return (
            jnp.where(low, first, pltpu.roll(second, 4, 1)),
            jnp.where(low, pltpu.roll(first, 4, 1), second),
        )

    def put(u, p, kt, block):
        first, second = [block[:, h * lanes:(h + 1) * lanes].reshape(groups, 8, lanes) for h in range(PAIR)]
        even, odd = swap(first, second)
        s_snd[u, p, :, :, span(kt)] = jnp.stack([even, odd], axis=1).reshape(planes, 8, lanes).astype(bf16)

    def take(u, p, kt):
        block = s_rcv[u, p, :, :, span(kt)].astype(f32).reshape(groups, 2, 8, lanes)
        first, second = swap(block[:, 0], block[:, 1])
        return jnp.concatenate([first.reshape(channels, lanes), second.reshape(channels, lanes)], axis=1)

    def turned(ref, p, kt):
        return jnp.concatenate([ref[p * PAIR + h, span(kt), :].astype(f32).T for h in range(PAIR)], axis=1)

    def same_of(p, kt):
        ids = chain_v[span(kt)].reshape(1, lanes)
        return jnp.concatenate([(ids == chain_s[me * rows + p * PAIR + h]).astype(f32) for h in range(PAIR)], axis=1)

    def mask_of(p, kt):
        pad = pad_v[span(kt)].reshape(1, lanes)
        return jnp.concatenate([(pad * pad_s[me * rows + p * PAIR + h]).astype(f32) for h in range(PAIR)], axis=1)

    def project(u, p, kt, sig_ref, lin_ref, first):
        blk = p * chunks + kt
        both = nn(wt_in[first:first + 2 * channels, :], z[blk])
        sig, lin = sigmoid(both[:channels]), both[channels:]
        sig_ref[blk] = sig
        lin_ref[blk] = lin
        put(u, p, kt, sig * lin * mask_of(p, kt))

    def turn_in(first):
        wt_in[first:first + channels, :] = w_in[:, first:first + channels].astype(f32).T.astype(bf16)

    turn_in(2 * channels)
    turn_in(3 * channels)
    bias_t[...] = jnp.broadcast_to(bias[...], (channels, channels)).T

    def start_block(p, kt):
        blk = p * chunks + kt
        col = bias_t[:, 0:1]
        values = turned(pair, p, kt) + same_of(p, kt) * col
        center = values - mean0(values)
        inverse = lax.rsqrt(mean0(center * center) + epsilon)
        z[blk] = (center * inverse).astype(bf16)
        rz[blk] = inverse
        project(B, p, kt, sig_b, lin_b, 2 * channels)

    @pl.loop(0, chunks)
    def _(kt):
        start_block(0, kt)

    pl.semaphore_wait(barrier, len(greeted))
    s_send(B, 0)

    @pl.loop(1, chunks)
    def _(p):
        @pl.loop(0, chunks)
        def _(kt):
            start_block(p, kt)

        s_send(B, p)

    turn_in(0)
    turn_in(channels)

    @pl.loop(0, chunks)
    def _(p):
        @pl.loop(0, chunks)
        def _(kt):
            project(A, p, kt, sig_a, lin_a, 0)

        s_send(A, p)

    i0 = lax.broadcasted_iota(jnp.int32, (size, size), 0)
    i1 = lax.broadcasted_iota(jnp.int32, (size, size), 1)

    def at_owner(i):
        return lax.rem(i, part) * mine + lax.div(i, part)

    gather[...] = (i1 == at_owner(i0)).astype(f32).astype(bf16)
    scatter[...] = (i0 == at_owner(i1)).astype(f32).astype(bf16)
    j0 = lax.broadcasted_iota(jnp.int32, (n, n), 0)
    j1 = lax.broadcasted_iota(jnp.int32, (n, n), 1)

    def natural(i):
        row, own = lax.rem(i, PAIR), lax.rem(lax.div(i, PAIR), planes)
        p, at = lax.rem(lax.div(i, part), chunks), lax.div(i, part * chunks)
        return (own * CORES + at) * rows + p * PAIR + row

    order[...] = (j0 == natural(j1)).astype(f32).astype(bf16)
    wt_gate[...] = w_gate[...].astype(f32).T.astype(bf16)
    wt_out[...] = w_out[...].astype(f32).T.astype(bf16)

    @pl.loop(0, chunks)
    def _(p):
        b_all[core, p] = to_channels(B, p).reshape(mine, part, n)
        remote(b_all.at[core, p], b_all.at[core, p], b_ssem.at[p], b_rsem.at[p], other)

        @pl.loop(0, chunks)
        def _(kt):
            blk = p * chunks + kt
            g = sigmoid(nn(wt_gate[...], z[blk]))
            cot = turned(gout, p, kt)
            gate[blk] = g
            gout_t[blk] = cot
            grad_u = (cot * g).astype(bf16)
            du[blk] = grad_u
            acc[blk] = nn(w_out[...], grad_u)

    @pl.loop(0, chunks)
    def _(p):
        wait(b_all.at[1 - core, p], b_rsem.at[p])

    @pl.loop(0, mine)
    def _(c):
        rows_b = jnp.concatenate([b_all[at, p, c] for at in range(CORES) for p in range(chunks)], axis=0)
        bn[c] = nn(order[...], rows_b).astype(bf16)

    @pl.loop(0, chunks)
    def _(p):
        ch_a[p] = to_channels(A, p).reshape(mine, part, n)
        got = jnp.concatenate([nt(ch_a[p, c], bn[c]).astype(bf16) for c in range(mine)], axis=0)
        to_rows(X, p, got)

    g_sum[...] = jnp.zeros_like(g_sum)
    chain_sum[...] = jnp.zeros_like(chain_sum)

    def add_sum(first, value):
        width = value.shape[1]
        g_sum[:, :, first:first + width] += value.reshape(quads, channels // quads, width)

    @pl.loop(0, chunks)
    def _(p):
        s_wait(X, p)

        @pl.loop(0, chunks)
        def _(kt):
            blk = p * chunks + kt
            values = take(X, p, kt)
            center = values - mean0(values)
            inverse = lax.rsqrt(mean0(center * center) + epsilon)
            normed = center * inverse
            xn[blk] = normed.astype(bf16)
            grad = acc[blk]
            grad = inverse * (grad - mean0(grad) - normed * mean0(grad * normed))
            put(DX, p, kt, grad)

        s_send(DX, p)

        @pl.loop(0, chunks)
        def _(kt):
            blk = p * chunks + kt
            lin = nn(wt_out[...], xn[blk])
            g = gate[blk]
            update_t[blk] = (g * lin).astype(bf16)
            grad_s = (gout_t[blk] * lin * g * (1.0 - g)).astype(bf16)
            ds[blk] = grad_s
            add_sum(4 * channels, nt(z[blk], grad_s))
            add_sum(5 * channels, nt(xn[blk], du[blk]))

    @pl.loop(0, chunks)
    def _(p):
        grad = to_channels(DX, p)
        ch_dxo[p] = nn(grad, order[...]).astype(bf16).reshape(mine, part, n)
        ch_dx[p] = grad.reshape(mine, part, n)
        got = jnp.concatenate([nn(ch_dx[p, c], bn[c]).astype(bf16) for c in range(mine)], axis=0)
        to_rows(DA, p, got)

    @pl.loop(0, mine)
    def _(c):
        left = jnp.concatenate([ch_dxo[p, c] for p in range(chunks)], axis=0)
        right = jnp.concatenate([ch_a[p, c] for p in range(chunks)], axis=0)
        db_part[c] = tn(left, right).reshape(CORES, chunks * part, n)
        db_snd[c] = db_part[c, 1 - core].astype(bf16)
        remote(db_snd.at[c], db_rcv.at[c], d_ssem.at[c], d_rsem.at[c], other)

    @pl.loop(0, mine)
    def _(c):
        wait(db_rcv.at[c], d_rsem.at[c])
        total = (db_part[c, core] + db_rcv[c].astype(f32)).astype(bf16)
        for p in range(chunks):
            ch_db[p, c] = total[p * part:(p + 1) * part]

    @pl.loop(0, chunks)
    def _(p):
        to_rows(DB, p, ch_db[p].reshape(size, n))

    def grad_project(u, p, kt, sig_ref, lin_ref, first):
        blk = p * chunks + kt
        sig = sig_ref[blk]
        grad = take(u, p, kt) * mask_of(p, kt) * sig
        both = jnp.concatenate([(grad * lin_ref[blk] * (1.0 - sig)).astype(bf16), grad.astype(bf16)], axis=0)
        add_sum(first, nt(z[blk], both))
        return nn(w_in[:, first:first + 2 * channels], both)

    @pl.loop(0, chunks)
    def _(p):
        s_wait(DA, p)

        @pl.loop(0, chunks)
        def _(kt):
            blk = p * chunks + kt
            acc[blk] = grad_project(DA, p, kt, sig_a, lin_a, 0) + nn(w_gate[...], ds[blk])

    @pl.loop(0, chunks)
    def _(p):
        s_wait(DB, p)

        @pl.loop(0, chunks)
        def _(kt):
            blk = p * chunks + kt
            grad = acc[blk] + grad_project(DB, p, kt, sig_b, lin_b, 2 * channels)
            normed = z[blk].astype(f32)
            grad = rz[blk] * (grad - mean0(grad) - normed * mean0(grad * normed))
            gpair_t[blk] = grad.astype(bf16)
            chain_sum[...] += grad * same_of(p, kt)

    total = jnp.sum(chain_sum[...], axis=1, keepdims=True)
    add_sum(6 * channels, jnp.broadcast_to(total, (channels, channels)))

    def send_quads(src, dst, step):
        for k in range(1, quads):
            to, device = quad_peer(k)
            remote(src(to), dst.at[quad], g_ssem.at[step], g_rsem.at[step], device)

    send_quads(lambda to: g_sum.at[to], g_rcv, 0)
    g_rcv[quad] = g_sum[quad]
    wait(g_rcv.at[pl.ds(0, quads - 1)], g_rsem.at[0])
    h_snd[...] = jnp.sum(g_rcv[...], axis=0)
    for k in range(1, QUAD):
        remote(h_snd, h_rcv.at[corner], g_ssem.at[1], g_rsem.at[1], corner_peer(k)[1])
    h_rcv[corner] = h_snd[...]
    wait(h_rcv.at[pl.ds(0, QUAD - 1)], g_rsem.at[1])
    o_snd[...] = jnp.sum(h_rcv[...], axis=0) * (1.0 / n)
    send_quads(lambda to: o_snd, sums, 2)
    sums[quad] = o_snd[...]
    wait(sums.at[pl.ds(0, quads - 1)], g_rsem.at[2])

    @pl.loop(0, 6)
    def _(u):
        @pl.loop(0, chunks)
        def _(p):
            wait(s_snd.at[u, p, pl.ds(0, planes - 1)], s_ssem.at[u, p])

    @pl.loop(0, chunks)
    def _(p):
        wait(b_all.at[core, p], b_ssem.at[p])

    @pl.loop(0, mine)
    def _(c):
        wait(db_snd.at[c], d_ssem.at[c])

    wait(g_sum.at[pl.ds(0, quads - 1)], g_ssem.at[0])
    wait(h_rcv.at[pl.ds(0, QUAD - 1)], g_ssem.at[1])
    wait(sums.at[pl.ds(0, quads - 1)], g_ssem.at[2])


def finish(update_t, gpair_t, sums, update, gpair, gw_in, gw_gate, gw_out, gw_chain):
    rows, n, channels = update.shape
    chunks = rows // PAIR
    lanes = n // chunks
    for src, dst in ((update_t, update), (gpair_t, gpair)):
        for p in range(chunks):
            for kt in range(chunks):
                block = src[p * chunks + kt].astype(f32)
                for h in range(PAIR):
                    turned = block[:, h * lanes:(h + 1) * lanes].T
                    dst[p * PAIR + h, kt * lanes:(kt + 1) * lanes, :] = turned.astype(bf16)
    gw_in[...] = sums[:, :, 0:4 * channels].reshape(channels, 4 * channels)
    gw_gate[...] = sums[:, :, 4 * channels:5 * channels].reshape(channels, channels)
    gw_out[...] = sums[:, :, 5 * channels:6 * channels].reshape(channels, channels)
    gw_chain[...] = sums[:, :, 6 * channels:7 * channels].reshape(channels, channels).T[0:1, :]


def on_device(devices, pair, grad_out, pad_mask, chain_ids, chain_bias, w_in, w_gate, w_out):
    rows, n, channels = pair.shape
    planes, quads = devices // CORES, devices // QUAD
    chunks = rows // PAIR
    lanes = n // chunks
    mine = channels // planes
    part = planes * PAIR
    size = part * mine
    blocks = chunks * chunks
    wide = PAIR * lanes
    per_quad = channels // quads
    columns = 7 * channels
    vmem, sems = pltpu.VMEM, pltpu.SemaphoreType.DMA
    scratch = [
        vmem((6, chunks, planes, PAIR * mine, n), bf16),
        vmem((6, chunks, planes, PAIR * mine, n), bf16),
        vmem((CORES, chunks, mine, part, n), bf16),
        vmem((chunks, mine, part, n), bf16),
        vmem((chunks, mine, part, n), bf16),
        vmem((chunks, mine, part, n), bf16),
        vmem((mine, CORES, chunks * part, n), f32),
        vmem((mine, chunks * part, n), bf16),
        vmem((mine, chunks * part, n), bf16),
        vmem((chunks, mine, part, n), bf16),
        vmem((blocks, channels, wide), bf16),
        vmem((blocks, 1, wide), f32),
        vmem((blocks, channels, wide), f32),
        vmem((blocks, channels, wide), f32),
        vmem((blocks, channels, wide), f32),
        vmem((blocks, channels, wide), f32),
        vmem((blocks, channels, wide), f32),
        vmem((blocks, channels, wide), f32),
        vmem((blocks, channels, wide), bf16),
        vmem((blocks, channels, wide), f32),
        vmem((blocks, channels, wide), bf16),
        vmem((blocks, channels, wide), bf16),
        vmem((channels, channels), f32),
        vmem((4 * channels, channels), bf16),
        vmem((channels, channels), bf16),
        vmem((channels, channels), bf16),
        vmem((size, size), bf16),
        vmem((size, size), bf16),
        vmem((n, n), bf16),
        vmem((mine, n, n), bf16),
        vmem((quads, per_quad, columns), f32),
        vmem((quads, per_quad, columns), f32),
        vmem((per_quad, columns), f32),
        vmem((QUAD, per_quad, columns), f32),
        vmem((per_quad, columns), f32),
        vmem((channels, wide), f32),
        sems((6, chunks)), sems((6, chunks)), sems((chunks,)), sems((chunks,)), sems((mine,)), sems((mine,)), sems((3,)), sems((3,)),
    ]
    in_vmem = pl.BlockSpec(memory_space=pltpu.VMEM)
    in_smem = pl.BlockSpec(memory_space=pltpu.SMEM)
    shape = jax.ShapeDtypeStruct
    update_t, gpair_t, sums = pl.pallas_call(
        functools.partial(kernel, devices),
        out_shape=(
            shape((blocks, channels, wide), bf16),
            shape((blocks, channels, wide), bf16),
            shape((quads, per_quad, columns), f32),
        ),
        in_specs=[in_vmem] * 4 + [in_smem] * 2 + [in_vmem] * 4,
        out_specs=[in_vmem] * 3,
        scratch_shapes=scratch,
        compiler_params=pltpu.CompilerParams(collective_id=0, has_side_effects=True, vmem_limit_bytes=56 * 2**20),
        cost_estimate=pl.CostEstimate(flops=2 * 10**9, bytes_accessed=3 * 10**6, transcendentals=10**6),
        name="exchange",
    )(pair, grad_out, pad_mask, chain_ids, pad_mask, chain_ids, chain_bias.reshape(1, channels), w_in, w_gate, w_out)
    out = pl.pallas_call(
        finish,
        out_shape=(
            shape(pair.shape, bf16),
            shape(pair.shape, bf16),
            shape(w_in.shape, f32),
            shape(w_gate.shape, f32),
            shape(w_out.shape, f32),
            shape((1, channels), f32),
        ),
        in_specs=[in_vmem] * 3,
        out_specs=[in_vmem] * 6,
        compiler_params=pltpu.CompilerParams(vmem_limit_bytes=32 * 2**20),
        cost_estimate=pl.CostEstimate(flops=10**6, bytes_accessed=4 * 10**6, transcendentals=0),
        name="finish",
    )(update_t, gpair_t, sums)
    return (*out[:5], out[5].reshape(channels))


def solution(mesh):
    placed = (P(("dp", "dap"), None, None), P(("dp", "dap"), None, None), P("dp"), P("dp"), P(), P(), P(), P())
    return jax.shard_map(
        functools.partial(on_device, mesh.shape["dap"]),
        mesh=mesh,
        in_specs=placed,
        out_specs=(
            P(("dp", "dap"), None, None),
            P(("dp", "dap"), None, None),
            P("dp", None),
            P("dp", None),
            P("dp", None),
            P("dp"),
        ),
        check_vma=False,
    )
```

```python
import functools

import jax
import jax.numpy as jnp
from jax import lax
from jax.experimental import pallas as pl
from jax.experimental.pallas import tpu as pltpu
from jax.sharding import PartitionSpec as P

epsilon = 1e-05
f32 = jnp.float32
bf16 = jnp.bfloat16

CORES = 2
PAIR = 2
B, A, X, DX, DA, DB = range(6)
EARLY, LATE = range(2)


def nn(left, right):
    return jnp.dot(left, right, preferred_element_type=f32)


def nt(left, right):
    return lax.dot_general(left, right, (((1,), (1,)), ((), ())), preferred_element_type=f32)


def tn(left, right):
    return lax.dot_general(left, right, (((0,), (0,)), ((), ())), preferred_element_type=f32)


def sigmoid(values):
    return 0.5 * jnp.tanh(0.5 * values) + 0.5


def mean0(values):
    return jnp.mean(values, axis=0, keepdims=True)


def kernel(
    devices,
    pair_hbm, gout_hbm, pad_hbm, chain_hbm, bias_hbm, w_in_hbm, w_gate_hbm, w_out_hbm,
    update, gpair, sums,
    pair, gout, pad_v, chain_v, pad_s, chain_s, bias, w_in, w_gate, w_out, in_sem,
    update_v, gpair_v, s_snd, s_rcv, b_all, ch_a, ch_dx, ch_dxo, db_part, db_snd, db_rcv, ch_db,
    z, rz, sig_a, lin_a, sig_b, lin_b, gate, gout_t, du, acc, xn, ds,
    bias_t, wt_in, wt_gate, wt_out, gather, scatter, order, bn,
    g_sum, g_rcv, rs_snd, rs_rcv, ag_snd,
    s_ssem, s_rsem, b_ssem, b_rsem, d_ssem, d_rsem, g_ssem, g_rsem, o_sem, own_sem,
):
    rows, n, channels = pair.shape
    planes = devices // CORES
    chunks = rows // PAIR
    lanes = n // chunks
    mine = channels // planes
    part = planes * PAIR
    size = part * mine
    me = lax.axis_index("dap")
    plane = lax.div(me, CORES)
    core = lax.rem(me, CORES)
    other = plane * CORES + 1 - core

    def plane_peer(k):
        to = lax.rem(plane + k, planes)
        return to, to * CORES + core

    barrier = pltpu.get_barrier_semaphore()
    greeted = [lax.rem(me + k, devices) for k in range(1, devices)]
    for device in greeted:
        pl.semaphore_signal(barrier, inc=1, device_id={"dap": device}, device_id_type=pl.DeviceIdType.MESH)

    loads = [
        pltpu.make_async_copy(src, dst, in_sem.at[i])
        for i, (src, dst) in enumerate((
            (pad_hbm, pad_v), (chain_hbm, chain_v), (pad_hbm, pad_s), (chain_hbm, chain_s), (bias_hbm, bias), (w_in_hbm, w_in),
            *((pair_hbm.at[pl.ds(p * PAIR, PAIR)], pair.at[pl.ds(p * PAIR, PAIR)]) for p in range(chunks)),
            (w_gate_hbm, w_gate), (w_out_hbm, w_out), (gout_hbm, gout),
        ))
    ]
    for load in loads:
        load.start()

    def loaded(count):
        for _ in range(count):
            loads.pop(0).wait()

    def remote(src, dst, ssem, rsem, device):
        pltpu.make_async_remote_copy(
            src_ref=src, dst_ref=dst, send_sem=ssem, recv_sem=rsem,
            device_id={"dap": device}, device_id_type=pl.DeviceIdType.MESH,
        ).start()

    def wait(ref, sem):
        pltpu.make_async_copy(ref, ref, sem).wait()

    def s_sent(step):
        wait(s_snd.at[0, 0, pl.ds(0, planes - 1)], s_ssem.at[step])

    def s_send(u, p):
        if u != B or p >= 2:
            s_sent(u * chunks + p - 2)
        for k in range(1, planes):
            to, device = plane_peer(k)
            remote(s_snd.at[u, p, to], s_rcv.at[u, p, plane], s_ssem.at[u * chunks + p], s_rsem.at[u, p], device)
        s_rcv[u, p, plane] = s_snd[u, p, plane]

    def s_wait(u, p):
        wait(s_rcv.at[u, p, pl.ds(0, planes - 1)], s_rsem.at[u, p])

    def to_channels(u, p):
        s_wait(u, p)
        return nn(gather[...], s_rcv[u, p].reshape(size, n)).astype(bf16)

    def to_rows(u, p, values):
        s_snd[u, p] = nn(scatter[...], values).astype(bf16).reshape(planes, PAIR * mine, n)
        s_send(u, p)

    def span(kt):
        return pl.ds(pl.multiple_of(kt * lanes, lanes), lanes)

    groups = channels // 8
    low = lax.broadcasted_iota(jnp.int32, (groups, 8, lanes), 1) < 4

    def swap(first, second):
        return (
            jnp.where(low, first, pltpu.roll(second, 4, 1)),
            jnp.where(low, pltpu.roll(first, 4, 1), second),
        )

    def put(u, p, kt, block):
        first, second = [block[:, h * lanes:(h + 1) * lanes].reshape(groups, 8, lanes) for h in range(PAIR)]
        even, odd = swap(first, second)
        s_snd[u, p, :, :, span(kt)] = jnp.stack([even, odd], axis=1).reshape(planes, 8, lanes).astype(bf16)

    def take(u, p, kt):
        block = s_rcv[u, p, :, :, span(kt)].astype(f32).reshape(groups, 2, 8, lanes)
        first, second = swap(block[:, 0], block[:, 1])
        return jnp.concatenate([first.reshape(channels, lanes), second.reshape(channels, lanes)], axis=1)

    def turned(ref, p, kt):
        return jnp.concatenate([ref[p * PAIR + h, span(kt), :].astype(f32).T for h in range(PAIR)], axis=1)

    def turn_back(ref, p, kt, block):
        for h in range(PAIR):
            ref[p * PAIR + h, span(kt), :] = block[:, h * lanes:(h + 1) * lanes].T.astype(bf16)

    def same_of(p, kt):
        ids = chain_v[span(kt)].reshape(1, lanes)
        return jnp.concatenate([(ids == chain_s[me * rows + p * PAIR + h]).astype(f32) for h in range(PAIR)], axis=1)

    def mask_of(p, kt):
        pad = pad_v[span(kt)].reshape(1, lanes)
        return jnp.concatenate([(pad * pad_s[me * rows + p * PAIR + h]).astype(f32) for h in range(PAIR)], axis=1)

    def project(u, p, kt, sig_ref, lin_ref, first):
        blk = p * chunks + kt
        both = nn(wt_in[first:first + 2 * channels, :], z[blk])
        sig, lin = sigmoid(both[:channels]), both[channels:]
        sig_ref[blk] = sig
        lin_ref[blk] = lin
        put(u, p, kt, sig * lin * mask_of(p, kt))

    def turn_in(first):
        wt_in[first:first + channels, :] = w_in[:, first:first + channels].astype(f32).T.astype(bf16)

    loaded(6)
    turn_in(2 * channels)
    turn_in(3 * channels)
    bias_t[...] = jnp.broadcast_to(bias[...], (channels, channels)).T

    def start_block(p, kt):
        blk = p * chunks + kt
        col = bias_t[:, 0:1]
        values = turned(pair, p, kt) + same_of(p, kt) * col
        center = values - mean0(values)
        inverse = lax.rsqrt(mean0(center * center) + epsilon)
        z[blk] = (center * inverse).astype(bf16)
        rz[blk] = inverse
        project(B, p, kt, sig_b, lin_b, 2 * channels)

    def start_chunk(p):
        loaded(1)

        @pl.loop(0, chunks)
        def _(kt):
            start_block(p, kt)

    def a_chunk(p):
        @pl.loop(0, chunks)
        def _(kt):
            project(A, p, kt, sig_a, lin_a, 0)

    def at_owner(i):
        return lax.rem(i, part) * mine + lax.div(i, part)

    def natural(i):
        row, own = lax.rem(i, PAIR), lax.rem(lax.div(i, PAIR), planes)
        p, at = lax.rem(lax.div(i, part), chunks), lax.div(i, part * chunks)
        return (own * CORES + at) * rows + p * PAIR + row

    def ones_at(down, along):
        return (down == along).astype(f32).astype(bf16)

    def down(k):
        return lax.broadcasted_iota(jnp.int32, (k, k), 0)

    def along(k):
        return lax.broadcasted_iota(jnp.int32, (1, k), 1)

    def pass_on(p):
        b_all[core, p] = to_channels(B, p).reshape(mine, part, n)
        remote(b_all.at[core, p], b_all.at[core, p], b_ssem.at[p], b_rsem.at[p], other)

    def gates(p):
        @pl.loop(0, chunks)
        def _(kt):
            blk = p * chunks + kt
            g = sigmoid(nn(wt_gate[...], z[blk]))
            cot = turned(gout, p, kt)
            gate[blk] = g
            gout_t[blk] = cot
            grad_u = (cot * g).astype(bf16)
            du[blk] = grad_u
            acc[blk] = nn(w_out[...], grad_u)

    start_chunk(0)
    pl.semaphore_wait(barrier, len(greeted))
    s_send(B, 0)
    start_chunk(1)
    s_send(B, 1)
    start_chunk(2)
    turn_in(0)
    turn_in(channels)
    a_chunk(0)
    s_send(B, 2)
    a_chunk(1)
    scatter[...] = ones_at(down(size), at_owner(along(size)))
    gather[...] = ones_at(lax.rem(down(size), part) * mine + lax.div(down(size), part), along(size))
    s_send(A, 0)
    pass_on(0)
    a_chunk(2)
    order[...] = ones_at(down(n), natural(along(n)))
    s_send(A, 1)
    pass_on(1)
    loaded(3)
    wt_gate[...] = w_gate[...].astype(f32).T.astype(bf16)
    wt_out[...] = w_out[...].astype(f32).T.astype(bf16)
    gates(0)
    s_send(A, 2)
    pass_on(2)

    @pl.loop(0, chunks)
    def _(p):
        wait(b_all.at[1 - core, p], b_rsem.at[p])

    @pl.loop(0, mine)
    def _(c):
        rows_b = jnp.concatenate([b_all[at, p, c] for at in range(CORES) for p in range(chunks)], axis=0)
        bn[c] = nn(order[...], rows_b).astype(bf16)

    @pl.loop(0, chunks)
    def _(p):
        ch_a[p] = to_channels(A, p).reshape(mine, part, n)
        got = jnp.concatenate([nt(ch_a[p, c], bn[c]).astype(bf16) for c in range(mine)], axis=0)
        to_rows(X, p, got)

    @pl.loop(1, chunks)
    def _(p):
        gates(p)

    def own(p):
        return pl.ds(p * PAIR, PAIR)

    g_sum[...] = jnp.zeros_like(g_sum)

    @pl.loop(0, chunks)
    def _(p):
        s_wait(X, p)

        @pl.loop(0, chunks)
        def _(kt):
            blk = p * chunks + kt
            values = take(X, p, kt)
            center = values - mean0(values)
            inverse = lax.rsqrt(mean0(center * center) + epsilon)
            normed = center * inverse
            xn[blk] = normed.astype(bf16)
            grad = acc[blk]
            grad = inverse * (grad - mean0(grad) - normed * mean0(grad * normed))
            put(DX, p, kt, grad)

        s_send(DX, p)

        @pl.loop(0, chunks)
        def _(kt):
            blk = p * chunks + kt
            lin = nn(wt_out[...], xn[blk])
            g = gate[blk]
            turn_back(update_v, p, kt, g * lin)
            grad_s = (gout_t[blk] * lin * g * (1.0 - g)).astype(bf16)
            ds[blk] = grad_s
            g_sum[EARLY, 1, :, :channels] += nt(z[blk], grad_s)
            g_sum[EARLY, 1, :, channels:] += nt(xn[blk], du[blk])

        pltpu.make_async_copy(update_v.at[own(p)], update.at[own(p)], o_sem.at[0, p]).start()

    @pl.loop(0, chunks)
    def _(p):
        grad = to_channels(DX, p)
        ch_dxo[p] = nn(grad, order[...]).astype(bf16).reshape(mine, part, n)
        ch_dx[p] = grad.reshape(mine, part, n)
        got = jnp.concatenate([nn(ch_dx[p, c], bn[c]).astype(bf16) for c in range(mine)], axis=0)
        to_rows(DA, p, got)

    @pl.loop(0, mine)
    def _(c):
        left = jnp.concatenate([ch_dxo[p, c] for p in range(chunks)], axis=0)
        right = jnp.concatenate([ch_a[p, c] for p in range(chunks)], axis=0)
        db_part[c] = tn(left, right).reshape(CORES, chunks * part, n)
        db_snd[c] = db_part[c, 1 - core].astype(bf16)
        remote(db_snd.at[c], db_rcv.at[c], d_ssem.at[c], d_rsem.at[c], other)

    @pl.loop(0, mine)
    def _(c):
        wait(db_rcv.at[c], d_rsem.at[c])
        total = (db_part[c, core] + db_rcv[c].astype(f32)).astype(bf16)
        for p in range(chunks):
            ch_db[p, c] = total[p * part:(p + 1) * part]

    @pl.loop(0, chunks)
    def _(p):
        to_rows(DB, p, ch_db[p].reshape(size, n))

    def grad_project(u, p, kt, sig_ref, lin_ref):
        blk = p * chunks + kt
        sig = sig_ref[blk]
        grad = take(u, p, kt) * mask_of(p, kt) * sig
        return jnp.concatenate([(grad * lin_ref[blk] * (1.0 - sig)).astype(bf16), grad.astype(bf16)], axis=0)

    @pl.loop(0, chunks)
    def _(p):
        s_wait(DA, p)

        @pl.loop(0, chunks)
        def _(kt):
            blk = p * chunks + kt
            both = grad_project(DA, p, kt, sig_a, lin_a)
            g_sum[EARLY, 0] += nt(z[blk], both)
            acc[blk] = nn(w_in[:, :2 * channels], both) + nn(w_gate[...], ds[blk])

    def sum_cores(group):
        remote(g_sum.at[group, 1 - core], g_rcv.at[group], g_ssem.at[group, 0], g_rsem.at[group, 0], other)

    def sum_planes(group):
        wait(g_rcv.at[group], g_rsem.at[group, 0])
        total = g_sum[group, core] + g_rcv[group]
        halves = [total[:, h * channels:(h + 1) * channels].reshape(groups, 8, channels) for h in range(2)]
        rs_snd[group] = jnp.stack(swap(*halves), axis=1).reshape(planes, 8, channels)
        for k in range(1, planes):
            to, device = plane_peer(k)
            remote(rs_snd.at[group, to], rs_rcv.at[group, plane], g_ssem.at[group, 1], g_rsem.at[group, 1], device)
        rs_rcv[group, plane] = rs_snd[group, plane]

    at_own = core * planes + plane

    def own_rows(group):
        return pltpu.make_async_copy(ag_snd.at[group], sums.at[group, at_own], own_sem.at[group])

    def share(group):
        wait(rs_rcv.at[group, pl.ds(0, planes - 1)], g_rsem.at[group, 1])
        ag_snd[group] = (jnp.sum(rs_rcv[group], axis=0) * (1.0 / n)).astype(bf16)
        for k in range(1, devices):
            device = lax.rem(me + k, devices)
            remote(ag_snd.at[group], sums.at[group, at_own], g_ssem.at[group, 2], g_rsem.at[group, 2], device)
        own_rows(group).start()

    def last_part(p):
        s_wait(DB, p)

        @pl.loop(0, chunks)
        def _(kt):
            blk = p * chunks + kt
            both = grad_project(DB, p, kt, sig_b, lin_b)
            added = nt(z[blk], both)
            g_sum[LATE, 0, :, :channels] += added[:, :channels]
            g_sum[LATE, 1, :, :channels] += added[:, channels:]
            grad = acc[blk] + nn(w_in[:, 2 * channels:], both)
            normed = z[blk].astype(f32)
            grad = rz[blk] * (grad - mean0(grad) - normed * mean0(grad * normed))
            turn_back(gpair_v, p, kt, grad)
            grad = grad * same_of(p, kt)
            g_sum[LATE, 0, :, channels:] += grad[:, :lanes]
            g_sum[LATE, 1, :, channels:] += grad[:, lanes:]

        pltpu.make_async_copy(gpair_v.at[own(p)], gpair.at[own(p)], o_sem.at[1, p]).start()

    sum_cores(EARLY)

    @pl.loop(0, chunks - 1)
    def _(p):
        last_part(p)

    s_sent(DB * chunks + chunks - 2)
    s_sent(DB * chunks + chunks - 1)
    sum_planes(EARLY)
    last_part(chunks - 1)
    sum_cores(LATE)
    sum_planes(LATE)
    share(EARLY)
    share(LATE)

    @pl.loop(0, chunks)
    def _(p):
        wait(b_all.at[core, p], b_ssem.at[p])

    @pl.loop(0, mine)
    def _(c):
        wait(db_snd.at[c], d_ssem.at[c])

    for group in (EARLY, LATE):
        wait(g_rcv.at[group], g_ssem.at[group, 0])
        wait(rs_snd.at[group, pl.ds(0, planes - 1)], g_ssem.at[group, 1])
        wait(sums.at[group, pl.ds(0, devices - 1)], g_ssem.at[group, 2])
        wait(sums.at[group, pl.ds(0, devices - 1)], g_rsem.at[group, 2])
        own_rows(group).wait()

    @pl.loop(0, chunks)
    def _(p):
        pltpu.make_async_copy(update_v.at[own(p)], update.at[own(p)], o_sem.at[0, p]).wait()
        pltpu.make_async_copy(gpair_v.at[own(p)], gpair.at[own(p)], o_sem.at[1, p]).wait()


def finish(
    update_hbm, gpair_hbm, sums_hbm, update, gpair, gw_in, gw_gate, gw_out, gw_chain,
    sums, update_v, gpair_v, in_v, gate_v, out_v, chain_v, sem, out_sem,
):
    rows, _, channels = update.shape
    groups = channels // 8
    loads, stores = [pltpu.make_async_copy(sums_hbm, sums, sem.at[0])], []

    def store(src, dst):
        stores.append(pltpu.make_async_copy(src, dst, out_sem.at[len(stores)]))
        return stores[-1]

    for src, mid, dst in ((update_hbm, update_v, update), (gpair_hbm, gpair_v, gpair)):
        for p in range(rows // PAIR):
            here = pl.ds(p * PAIR, PAIR)
            loads.append(pltpu.make_async_copy(src.at[here], mid.at[here], sem.at[len(loads)]))
            store(mid.at[here], dst.at[here])
    for load in loads:
        load.start()
    loads[0].wait()
    low = lax.broadcasted_iota(jnp.int32, (groups, 8, channels), 1) < 4

    def whole(group, at):
        planes = sums.shape[1] // CORES
        block = sums[group, at * planes:(at + 1) * planes].astype(f32).reshape(groups, 2, 8, channels)
        even, odd = block[:, 0], block[:, 1]
        first = jnp.where(low, even, pltpu.roll(odd, 4, 1))
        second = jnp.where(low, pltpu.roll(even, 4, 1), odd)
        return first.reshape(channels, channels), second.reshape(channels, channels)

    for load, out in zip(loads[1:], list(stores)):
        load.wait()
        out.start()
    gate_a, lin_a = whole(EARLY, 0)
    gate_v[...], out_v[...] = whole(EARLY, 1)
    gate_b, chain_0 = whole(LATE, 0)
    lin_b, chain_1 = whole(LATE, 1)
    for i, part in enumerate((gate_a, lin_a, gate_b, lin_b)):
        in_v[:, i * channels:(i + 1) * channels] = part
    chain_v[...] = jnp.sum((chain_0 + chain_1).T, axis=0, keepdims=True)
    for src, dst in ((in_v, gw_in), (gate_v, gw_gate), (out_v, gw_out), (chain_v, gw_chain)):
        store(src, dst).start()
    for out in stores:
        out.wait()


def on_device(devices, pair, grad_out, pad_mask, chain_ids, chain_bias, w_in, w_gate, w_out):
    rows, n, channels = pair.shape
    planes = devices // CORES
    chunks = rows // PAIR
    lanes = n // chunks
    mine = channels // planes
    part = planes * PAIR
    size = part * mine
    blocks = chunks * chunks
    wide = PAIR * lanes
    vmem, sems = pltpu.VMEM, pltpu.SemaphoreType.DMA
    scratch = [
        vmem(pair.shape, bf16),
        vmem(pair.shape, bf16),
        vmem((n,), jnp.int32),
        vmem((n,), jnp.int32),
        pltpu.SMEM((n,), jnp.int32),
        pltpu.SMEM((n,), jnp.int32),
        vmem((1, channels), f32),
        vmem(w_in.shape, bf16),
        vmem(w_gate.shape, bf16),
        vmem(w_out.shape, bf16),
        sems((9 + chunks,)),
        vmem(pair.shape, bf16),
        vmem(pair.shape, bf16),
        vmem((6, chunks, planes, PAIR * mine, n), bf16),
        vmem((6, chunks, planes, PAIR * mine, n), bf16),
        vmem((CORES, chunks, mine, part, n), bf16),
        vmem((chunks, mine, part, n), bf16),
        vmem((chunks, mine, part, n), bf16),
        vmem((chunks, mine, part, n), bf16),
        vmem((mine, CORES, chunks * part, n), f32),
        vmem((mine, chunks * part, n), bf16),
        vmem((mine, chunks * part, n), bf16),
        vmem((chunks, mine, part, n), bf16),
        vmem((blocks, channels, wide), bf16),
        vmem((blocks, 1, wide), f32),
        vmem((blocks, channels, wide), f32),
        vmem((blocks, channels, wide), f32),
        vmem((blocks, channels, wide), f32),
        vmem((blocks, channels, wide), f32),
        vmem((blocks, channels, wide), f32),
        vmem((blocks, channels, wide), f32),
        vmem((blocks, channels, wide), bf16),
        vmem((blocks, channels, wide), f32),
        vmem((blocks, channels, wide), bf16),
        vmem((blocks, channels, wide), bf16),
        vmem((channels, channels), f32),
        vmem((4 * channels, channels), bf16),
        vmem((channels, channels), bf16),
        vmem((channels, channels), bf16),
        vmem((size, size), bf16),
        vmem((size, size), bf16),
        vmem((n, n), bf16),
        vmem((mine, n, n), bf16),
        vmem((2, CORES, channels, 2 * channels), f32),
        vmem((2, channels, 2 * channels), f32),
        vmem((2, planes, 8, channels), f32),
        vmem((2, planes, 8, channels), f32),
        vmem((2, 8, channels), bf16),
        sems((6 * chunks,)), sems((6, chunks)), sems((chunks,)), sems((chunks,)), sems((mine,)), sems((mine,)),
        sems((2, 3)), sems((2, 3)), sems((2, chunks)), sems((2,)),
    ]
    in_any = pl.BlockSpec(memory_space=pl.ANY)
    shape = jax.ShapeDtypeStruct
    update, gpair, sums = pl.pallas_call(
        functools.partial(kernel, devices),
        out_shape=(
            shape(pair.shape, bf16),
            shape(pair.shape, bf16),
            shape((2, devices, 8, channels), bf16),
        ),
        in_specs=[in_any] * 8,
        out_specs=[in_any] * 3,
        scratch_shapes=scratch,
        compiler_params=pltpu.CompilerParams(collective_id=0, has_side_effects=True, vmem_limit_bytes=56 * 2**20),
        cost_estimate=pl.CostEstimate(flops=2 * 10**9, bytes_accessed=3 * 10**6, transcendentals=10**6),
        name="exchange",
    )(pair, grad_out, pad_mask, chain_ids, chain_bias.reshape(1, channels), w_in, w_gate, w_out)
    out = pl.pallas_call(
        finish,
        out_shape=(
            shape(pair.shape, bf16),
            shape(pair.shape, bf16),
            shape(w_in.shape, f32),
            shape(w_gate.shape, f32),
            shape(w_out.shape, f32),
            shape((1, channels), f32),
        ),
        in_specs=[in_any] * 3,
        out_specs=[in_any] * 6,
        scratch_shapes=[
            vmem((2, devices, 8, channels), bf16), vmem(pair.shape, bf16), vmem(pair.shape, bf16),
            vmem(w_in.shape, f32), vmem(w_gate.shape, f32), vmem(w_out.shape, f32), vmem((1, channels), f32),
            sems((1 + 2 * chunks,)), sems((4 + 2 * chunks,)),
        ],
        compiler_params=pltpu.CompilerParams(vmem_limit_bytes=56 * 2**20),
        cost_estimate=pl.CostEstimate(flops=10**6, bytes_accessed=4 * 10**6, transcendentals=0),
        name="finish",
    )(update, gpair, sums)
    return (*out[:5], out[5].reshape(channels))


def solution(mesh):
    placed = (P(("dp", "dap"), None, None), P(("dp", "dap"), None, None), P("dp"), P("dp"), P(), P(), P(), P())
    return jax.shard_map(
        functools.partial(on_device, mesh.shape["dap"]),
        mesh=mesh,
        in_specs=placed,
        out_specs=(
            P(("dp", "dap"), None, None),
            P(("dp", "dap"), None, None),
            P("dp", None),
            P("dp", None),
            P("dp", None),
            P("dp"),
        ),
        check_vma=False,
    )
```

```python
import functools

import jax
import jax.numpy as jnp
from jax import lax
from jax.experimental import pallas as pl
from jax.experimental.pallas import tpu as pltpu
from jax.sharding import PartitionSpec as P

epsilon = 1e-05
f32 = jnp.float32
bf16 = jnp.bfloat16

CORES = 2
PAIR = 2
B, A, X, DX, DA, DB = range(6)
EARLY, LATE = range(2)


def nn(left, right):
    return jnp.dot(left, right, preferred_element_type=f32)


def nt(left, right):
    return lax.dot_general(left, right, (((1,), (1,)), ((), ())), preferred_element_type=f32)


def tn(left, right):
    return lax.dot_general(left, right, (((0,), (0,)), ((), ())), preferred_element_type=f32)


def sigmoid(values):
    return 0.5 * jnp.tanh(0.5 * values) + 0.5


def mean0(values):
    return jnp.mean(values, axis=0, keepdims=True)


def kernel(
    devices,
    pair_hbm, gout_hbm, pad_hbm, chain_hbm, bias_hbm, w_in_hbm, w_gate_hbm, w_out_hbm,
    update, gpair, sums_early, sums_late, chain_out,
    pair, gout, pad_v, chain_v, pad_s, chain_s, bias, w_in, w_gate, w_out, in_sem,
    update_v, gpair_v, s_snd, s_rcv, b_all, ch_a, ch_dx, db_part, db_snd, db_rcv, ch_db,
    z, rz, sig_a, lin_a, sig_b, lin_b, gate, gout_t, du, acc, xn, ds,
    bias_t, wt_in, wt_gate, wt_out, gather, scatter, order, order_t,
    g_early, g_late, both_v, chain_sum, chain_snd, chain_rcv, chain_own, chain_other, chain_all,
    core_early, core_late, rs_early, rs_late, got_early, got_late, ag_early, ag_late,
    s_ssem, s_rsem, b_ssem, b_rsem, d_ssem, d_rsem, g_ssem, g_rsem, o_sem, own_sem, c_sem,
):
    rows, n, channels = pair.shape
    planes = devices // CORES
    chunks = rows // PAIR
    lanes = n // chunks
    mine = channels // planes
    part = planes * PAIR
    size = part * mine
    me = lax.axis_index("dap")
    plane = lax.div(me, CORES)
    core = lax.rem(me, CORES)
    other = plane * CORES + 1 - core

    side = 4 if planes == 32 else 2
    offsets = [(dz, dy, dx) for dz in range(side) for dy in range(side) for dx in range(2)]
    offsets.sort(key=lambda o: -(min(o[0], side - o[0]) + min(o[1], side - o[1]) + o[2]))
    at_z, at_y, at_x = lax.div(plane, 2 * side), lax.rem(lax.div(plane, 2), side), lax.rem(plane, 2)

    def plane_peer(k):
        dz, dy, dx = offsets[k - 1]
        to = (lax.rem(at_z + dz, side) * side + lax.rem(at_y + dy, side)) * 2 + lax.rem(at_x + dx, 2)
        return to, to * CORES + core

    barrier = pltpu.get_barrier_semaphore()
    greeted = [plane_peer(k)[1] for k in range(1, planes)] + [other]
    for device in greeted:
        pl.semaphore_signal(barrier, inc=1, device_id={"dap": device}, device_id_type=pl.DeviceIdType.MESH)

    loads = [
        pltpu.make_async_copy(src, dst, in_sem.at[i])
        for i, (src, dst) in enumerate((
            (pad_hbm, pad_v), (chain_hbm, chain_v), (pad_hbm, pad_s), (chain_hbm, chain_s), (bias_hbm, bias), (w_in_hbm, w_in),
            *((pair_hbm.at[pl.ds(p * PAIR, PAIR)], pair.at[pl.ds(p * PAIR, PAIR)]) for p in range(chunks)),
            (w_gate_hbm, w_gate), (w_out_hbm, w_out), (gout_hbm, gout),
        ))
    ]
    for load in loads:
        load.start()

    def loaded(count):
        for _ in range(count):
            loads.pop(0).wait()

    def remote(src, dst, ssem, rsem, device):
        pltpu.make_async_remote_copy(
            src_ref=src, dst_ref=dst, send_sem=ssem, recv_sem=rsem,
            device_id={"dap": device}, device_id_type=pl.DeviceIdType.MESH,
        ).start()

    def wait(ref, sem):
        pltpu.make_async_copy(ref, ref, sem).wait()

    def s_sent(step):
        wait(s_snd.at[0, 0, pl.ds(0, planes - 1)], s_ssem.at[step])

    def s_send(u, p):
        if u != B or p >= 2:
            s_sent(u * chunks + p - 2)
        for k in range(1, planes):
            to, device = plane_peer(k)
            remote(s_snd.at[u, p, to], s_rcv.at[u, p, plane], s_ssem.at[u * chunks + p], s_rsem.at[u, p], device)
        s_rcv[u, p, plane] = s_snd[u, p, plane]

    def s_wait(u, p):
        wait(s_rcv.at[u, p, pl.ds(0, planes - 1)], s_rsem.at[u, p])

    def to_channels(u, p):
        s_wait(u, p)
        return nn(gather[...], s_rcv[u, p].reshape(size, n)).astype(bf16)

    def to_rows(u, p, values):
        s_snd[u, p] = nn(scatter[...], values).astype(bf16).reshape(planes, PAIR * mine, n)
        s_send(u, p)

    def span(kt):
        return pl.ds(pl.multiple_of(kt * lanes, lanes), lanes)

    groups = channels // 8
    low = lax.broadcasted_iota(jnp.int32, (groups, 8, lanes), 1) < 4

    def swap(first, second):
        return (
            jnp.where(low, first, pltpu.roll(second, 4, 1)),
            jnp.where(low, pltpu.roll(first, 4, 1), second),
        )

    def put(u, p, kt, block):
        first, second = [block[:, h * lanes:(h + 1) * lanes].reshape(groups, 8, lanes) for h in range(PAIR)]
        even, odd = swap(first, second)
        s_snd[u, p, :, :, span(kt)] = jnp.stack([even, odd], axis=1).reshape(planes, 8, lanes).astype(bf16)

    def take(u, p, kt):
        block = s_rcv[u, p, :, :, span(kt)].astype(f32).reshape(groups, 2, 8, lanes)
        first, second = swap(block[:, 0], block[:, 1])
        return jnp.concatenate([first.reshape(channels, lanes), second.reshape(channels, lanes)], axis=1)

    def turned(ref, p, kt):
        return jnp.concatenate([ref[p * PAIR + h, span(kt), :].astype(f32).T for h in range(PAIR)], axis=1)

    def turn_back(ref, p, kt, block):
        for h in range(PAIR):
            ref[p * PAIR + h, span(kt), :] = block[:, h * lanes:(h + 1) * lanes].T.astype(bf16)

    def same_of(p, kt):
        ids = chain_v[span(kt)].reshape(1, lanes)
        return jnp.concatenate([(ids == chain_s[me * rows + p * PAIR + h]).astype(f32) for h in range(PAIR)], axis=1)

    def mask_of(p, kt):
        pad = pad_v[span(kt)].reshape(1, lanes)
        return jnp.concatenate([(pad * pad_s[me * rows + p * PAIR + h]).astype(f32) for h in range(PAIR)], axis=1)

    def project(u, p, kt, sig_ref, lin_ref, first):
        blk = p * chunks + kt
        both = nn(wt_in[first:first + 2 * channels, :], z[blk])
        sig, lin = sigmoid(both[:channels]), both[channels:]
        sig_ref[blk] = sig
        lin_ref[blk] = lin
        put(u, p, kt, sig * lin * mask_of(p, kt))

    def turn_in(first):
        wt_in[first:first + channels, :] = w_in[:, first:first + channels].astype(f32).T.astype(bf16)

    loaded(6)
    turn_in(2 * channels)
    turn_in(3 * channels)
    bias_t[...] = jnp.broadcast_to(bias[...], (channels, channels)).T

    def start_block(p, kt):
        blk = p * chunks + kt
        col = bias_t[:, 0:1]
        values = turned(pair, p, kt) + same_of(p, kt) * col
        center = values - mean0(values)
        inverse = lax.rsqrt(mean0(center * center) + epsilon)
        z[blk] = (center * inverse).astype(bf16)
        rz[blk] = inverse
        project(B, p, kt, sig_b, lin_b, 2 * channels)

    def start_chunk(p):
        loaded(1)

        @pl.loop(0, chunks)
        def _(kt):
            start_block(p, kt)

    def a_chunk(p):
        @pl.loop(0, chunks)
        def _(kt):
            project(A, p, kt, sig_a, lin_a, 0)

    def at_owner(i):
        return lax.rem(i, part) * mine + lax.div(i, part)

    def natural(i):
        row, own = lax.rem(i, PAIR), lax.rem(lax.div(i, PAIR), planes)
        p, at = lax.rem(lax.div(i, part), chunks), lax.div(i, part * chunks)
        return (own * CORES + at) * rows + p * PAIR + row

    def ones_at(down, along):
        return (down == along).astype(f32).astype(bf16)

    def down(k):
        return lax.broadcasted_iota(jnp.int32, (k, 1), 0)

    def along(k):
        return lax.broadcasted_iota(jnp.int32, (1, k), 1)

    def pass_on(p):
        b_all[:, core, p] = to_channels(B, p).reshape(mine, part, n)
        here = b_all.at[:, core, p]
        remote(here, here, b_ssem.at[p], b_rsem.at[p], other)

    def gates(p):
        @pl.loop(0, chunks)
        def _(kt):
            blk = p * chunks + kt
            g = sigmoid(nn(wt_gate[...], z[blk]))
            cot = turned(gout, p, kt)
            gate[blk] = g
            gout_t[blk] = cot
            grad_u = (cot * g).astype(bf16)
            du[blk] = grad_u
            acc[blk] = nn(w_out[...], grad_u)

    start_chunk(0)
    pl.semaphore_wait(barrier, len(greeted))
    s_send(B, 0)
    start_chunk(1)
    s_send(B, 1)
    start_chunk(2)
    turn_in(0)
    turn_in(channels)
    a_chunk(0)
    s_send(B, 2)
    a_chunk(1)
    scatter[...] = ones_at(down(size), at_owner(along(size)))
    gather[...] = ones_at(lax.rem(down(size), part) * mine + lax.div(down(size), part), along(size))
    pass_on(0)
    s_send(A, 0)
    a_chunk(2)
    order[...] = ones_at(down(n), natural(along(n)))
    order_t[...] = ones_at(natural(down(n)), along(n))
    pass_on(1)
    s_send(A, 1)
    loaded(3)
    wt_gate[...] = w_gate[...].astype(f32).T.astype(bf16)
    wt_out[...] = w_out[...].astype(f32).T.astype(bf16)
    gates(0)
    pass_on(2)
    s_send(A, 2)

    @pl.loop(0, chunks)
    def _(p):
        wait(b_all.at[:, 1 - core, p], b_rsem.at[p])

    def b_of(c):
        return b_all[c].reshape(n, n)

    @pl.loop(0, chunks)
    def _(p):
        ch_a[p] = to_channels(A, p).reshape(mine, part, n)
        got = jnp.concatenate([nt(ch_a[p, c], b_of(c)).astype(bf16) for c in range(mine)], axis=0)
        to_rows(X, p, nn(got, order_t[...]).astype(bf16))

    @pl.loop(1, chunks)
    def _(p):
        gates(p)

    def own(p):
        return pl.ds(p * PAIR, PAIR)

    g_early[...] = jnp.zeros_like(g_early)
    g_late[...] = jnp.zeros_like(g_late)
    chain_sum[...] = jnp.zeros_like(chain_sum)

    @pl.loop(0, chunks)
    def _(p):
        s_wait(X, p)

        @pl.loop(0, chunks)
        def _(kt):
            blk = p * chunks + kt
            values = take(X, p, kt)
            center = values - mean0(values)
            inverse = lax.rsqrt(mean0(center * center) + epsilon)
            normed = center * inverse
            xn[blk] = normed.astype(bf16)
            grad = acc[blk]
            grad = inverse * (grad - mean0(grad) - normed * mean0(grad * normed))
            put(DX, p, kt, grad)

        s_send(DX, p)

        @pl.loop(0, chunks)
        def _(kt):
            blk = p * chunks + kt
            lin = nn(wt_out[...], xn[blk])
            g = gate[blk]
            turn_back(update_v, p, kt, g * lin)
            grad_s = (gout_t[blk] * lin * g * (1.0 - g)).astype(bf16)
            ds[blk] = grad_s
            g_early[1, :, :channels] += nt(z[blk], grad_s)
            g_early[1, :, channels:] += nt(xn[blk], du[blk])

        pltpu.make_async_copy(update_v.at[own(p)], update.at[own(p)], o_sem.at[0, p]).start()

    @pl.loop(0, chunks)
    def _(p):
        ch_dx[p] = nn(to_channels(DX, p), order[...]).astype(bf16).reshape(mine, part, n)
        got = jnp.concatenate([nn(ch_dx[p, c], b_of(c)).astype(bf16) for c in range(mine)], axis=0)
        to_rows(DA, p, got)

    @pl.loop(0, mine)
    def _(c):
        left = jnp.concatenate([ch_dx[p, c] for p in range(chunks)], axis=0)
        right = jnp.concatenate([ch_a[p, c] for p in range(chunks)], axis=0)
        db_part[c] = tn(left, right).reshape(CORES, chunks * part, n)
        db_snd[c] = db_part[c, 1 - core].astype(bf16)
        remote(db_snd.at[c], db_rcv.at[c], d_ssem.at[c], d_rsem.at[c], other)

    @pl.loop(0, mine)
    def _(c):
        wait(db_rcv.at[c], d_rsem.at[c])
        total = (db_part[c, core] + db_rcv[c].astype(f32)).astype(bf16)
        for p in range(chunks):
            ch_db[p, c] = total[p * part:(p + 1) * part]

    @pl.loop(0, chunks)
    def _(p):
        to_rows(DB, p, ch_db[p].reshape(size, n))

    def grad_project(u, p, kt, sig_ref, lin_ref):
        blk = p * chunks + kt
        sig = sig_ref[blk]
        grad = take(u, p, kt) * mask_of(p, kt) * sig
        return jnp.concatenate([(grad * lin_ref[blk] * (1.0 - sig)).astype(bf16), grad.astype(bf16)], axis=0)

    @pl.loop(0, chunks)
    def _(p):
        s_wait(DA, p)

        @pl.loop(0, chunks)
        def _(kt):
            blk = p * chunks + kt
            both = grad_project(DA, p, kt, sig_a, lin_a)
            g_early[0] += nt(z[blk], both)
            acc[blk] = nn(w_in[:, :2 * channels], both) + nn(w_gate[...], ds[blk])

    grads = (g_early, g_late)
    cores = (core_early, core_late)
    rs_snd, rs_rcv = (rs_early, rs_late), (got_early, got_late)
    ag_snd, sums = (ag_early, ag_late), (sums_early, sums_late)
    others = pl.ds(0, planes - 1)

    def send_rows(src, dst, group, step):
        for k in range(1, planes):
            to, device = plane_peer(k)
            remote(src(to), dst.at[plane], g_ssem.at[group, step], g_rsem.at[group, step], device)

    def sum_planes(group):
        tiles = []
        for at in range(grads[group].shape[0]):
            halves = [grads[group][at, :, h * channels:(h + 1) * channels].reshape(groups, 8, channels) for h in range(2)]
            tiles.append(jnp.stack(swap(*halves), axis=1).reshape(planes, 8, channels))
        rs_snd[group][...] = jnp.concatenate(tiles, axis=1).astype(bf16)
        send_rows(lambda to: rs_snd[group].at[to], rs_rcv[group], group, 0)
        rs_rcv[group][plane] = rs_snd[group][plane]

    def sum_cores(group):
        wait(rs_rcv[group].at[others], g_rsem.at[group, 0])
        cores[group][0] = jnp.sum(rs_rcv[group][...].astype(f32), axis=0) * (1.0 / n)
        remote(cores[group].at[0], cores[group].at[1], g_ssem.at[group, 1], g_rsem.at[group, 1], other)

    own_rows = [pltpu.make_async_copy(ag_snd[group], sums[group].at[plane], own_sem.at[group]) for group in (EARLY, LATE)]

    def share(group):
        wait(cores[group].at[1], g_rsem.at[group, 1])
        ag_snd[group][...] = (cores[group][0] + cores[group][1]).astype(bf16)
        send_rows(lambda to: ag_snd[group], sums[group], group, 2)
        own_rows[group].start()

    def last_sums(p):
        s_wait(DB, p)

        @pl.loop(0, chunks)
        def _(kt):
            both = grad_project(DB, p, kt, sig_b, lin_b)
            both_v[kt] = both
            g_late[0] += nt(z[p * chunks + kt], both)

    def last_grads(p):
        @pl.loop(0, chunks)
        def _(kt):
            blk = p * chunks + kt
            grad = acc[blk] + nn(w_in[:, 2 * channels:], both_v[kt])
            normed = z[blk].astype(f32)
            grad = rz[blk] * (grad - mean0(grad) - normed * mean0(grad * normed))
            turn_back(gpair_v, p, kt, grad)
            grad = grad * same_of(p, kt)
            chain_sum[...] += grad[:, :lanes] + grad[:, lanes:]

        pltpu.make_async_copy(gpair_v.at[own(p)], gpair.at[own(p)], o_sem.at[1, p]).start()

    @pl.loop(0, chunks - 2)
    def _(p):
        last_sums(p)
        last_grads(p)

    s_sent(DB * chunks + chunks - 2)
    s_sent(DB * chunks + chunks - 1)
    sum_planes(EARLY)
    last_sums(chunks - 2)
    last_grads(chunks - 2)
    last_sums(chunks - 1)
    sum_planes(LATE)
    last_grads(chunks - 1)
    chain_snd[...] = jnp.sum(chain_sum[...].T, axis=0, keepdims=True)
    for k in range(1, planes):
        remote(chain_snd, chain_rcv.at[plane], c_sem.at[0], c_sem.at[1], plane_peer(k)[1])
    chain_rcv[plane] = chain_snd[...]
    sum_cores(EARLY)
    share(EARLY)
    sum_cores(LATE)
    wait(chain_rcv.at[others], c_sem.at[1])
    chain_own[...] = jnp.sum(chain_rcv[...], axis=0) * (1.0 / n)
    remote(chain_own, chain_other, c_sem.at[2], c_sem.at[3], other)
    share(LATE)
    wait(chain_other, c_sem.at[3])
    chain_all[...] = chain_own[...] + chain_other[...]
    chain_copy = pltpu.make_async_copy(chain_all, chain_out, c_sem.at[4])
    chain_copy.start()

    @pl.loop(0, chunks)
    def _(p):
        wait(b_all.at[:, core, p], b_ssem.at[p])

    @pl.loop(0, mine)
    def _(c):
        wait(db_snd.at[c], d_ssem.at[c])

    for group in (EARLY, LATE):
        wait(rs_snd[group].at[others], g_ssem.at[group, 0])
        wait(cores[group].at[0], g_ssem.at[group, 1])
        wait(sums[group].at[others], g_ssem.at[group, 2])
        wait(sums[group].at[others], g_rsem.at[group, 2])
        own_rows[group].wait()

    wait(chain_rcv.at[others], c_sem.at[0])
    wait(chain_own, c_sem.at[2])
    chain_copy.wait()

    @pl.loop(0, chunks)
    def _(p):
        pltpu.make_async_copy(update_v.at[own(p)], update.at[own(p)], o_sem.at[0, p]).wait()
        pltpu.make_async_copy(gpair_v.at[own(p)], gpair.at[own(p)], o_sem.at[1, p]).wait()


def finish(
    update_hbm, gpair_hbm, early_hbm, late_hbm, chain_hbm, update, gpair, gw_in, gw_gate, gw_out, gw_chain,
    early, late, update_v, gpair_v, in_v, gate_v, out_v, chain_v, sem, out_sem,
):
    rows, _, channels = update.shape
    groups = channels // 8
    loads, stores = [], []
    for src, dst in ((early_hbm, early), (late_hbm, late), (chain_hbm, chain_v)):
        loads.append(pltpu.make_async_copy(src, dst, sem.at[len(loads)]))

    def store(src, dst):
        stores.append(pltpu.make_async_copy(src, dst, out_sem.at[len(stores)]))
        return stores[-1]

    for src, mid, dst in ((update_hbm, update_v, update), (gpair_hbm, gpair_v, gpair)):
        for p in range(rows // PAIR):
            here = pl.ds(p * PAIR, PAIR)
            loads.append(pltpu.make_async_copy(src.at[here], mid.at[here], sem.at[len(loads)]))
            store(mid.at[here], dst.at[here])
    for load in loads:
        load.start()
    low = lax.broadcasted_iota(jnp.int32, (groups, 8, channels), 1) < 4

    def whole(sums, at):
        block = sums[...].astype(f32)[:, at * 8:(at + 1) * 8].reshape(groups, 2, 8, channels)
        even, odd = block[:, 0], block[:, 1]
        first = jnp.where(low, even, pltpu.roll(odd, 4, 1))
        second = jnp.where(low, pltpu.roll(even, 4, 1), odd)
        return first.reshape(channels, channels), second.reshape(channels, channels)

    for load, out in zip(loads[3:], list(stores)):
        load.wait()
        out.start()
    for load in loads[:3]:
        load.wait()
    store(chain_v, gw_chain).start()
    gate_v[...], out_v[...] = whole(early, 1)
    for i, part in enumerate(whole(early, 0) + whole(late, 0)):
        in_v[:, i * channels:(i + 1) * channels] = part
    for src, dst in ((in_v, gw_in), (gate_v, gw_gate), (out_v, gw_out)):
        store(src, dst).start()
    for out in stores:
        out.wait()


def on_device(devices, pair, grad_out, pad_mask, chain_ids, chain_bias, w_in, w_gate, w_out):
    rows, n, channels = pair.shape
    planes = devices // CORES
    chunks = rows // PAIR
    lanes = n // chunks
    mine = channels // planes
    part = planes * PAIR
    size = part * mine
    blocks = chunks * chunks
    wide = PAIR * lanes
    vmem, sems = pltpu.VMEM, pltpu.SemaphoreType.DMA
    scratch = [
        vmem(pair.shape, bf16),
        vmem(pair.shape, bf16),
        vmem((n,), jnp.int32),
        vmem((n,), jnp.int32),
        pltpu.SMEM((n,), jnp.int32),
        pltpu.SMEM((n,), jnp.int32),
        vmem((1, channels), f32),
        vmem(w_in.shape, bf16),
        vmem(w_gate.shape, bf16),
        vmem(w_out.shape, bf16),
        sems((9 + chunks,)),
        vmem(pair.shape, bf16),
        vmem(pair.shape, bf16),
        vmem((6, chunks, planes, PAIR * mine, n), bf16),
        vmem((6, chunks, planes, PAIR * mine, n), bf16),
        vmem((mine, CORES, chunks, part, n), bf16),
        vmem((chunks, mine, part, n), bf16),
        vmem((chunks, mine, part, n), bf16),
        vmem((mine, CORES, chunks * part, n), f32),
        vmem((mine, chunks * part, n), bf16),
        vmem((mine, chunks * part, n), bf16),
        vmem((chunks, mine, part, n), bf16),
        vmem((blocks, channels, wide), bf16),
        vmem((blocks, 1, wide), f32),
        vmem((blocks, channels, wide), f32),
        vmem((blocks, channels, wide), f32),
        vmem((blocks, channels, wide), f32),
        vmem((blocks, channels, wide), f32),
        vmem((blocks, channels, wide), f32),
        vmem((blocks, channels, wide), f32),
        vmem((blocks, channels, wide), bf16),
        vmem((blocks, channels, wide), f32),
        vmem((blocks, channels, wide), bf16),
        vmem((blocks, channels, wide), bf16),
        vmem((channels, channels), f32),
        vmem((4 * channels, channels), bf16),
        vmem((channels, channels), bf16),
        vmem((channels, channels), bf16),
        vmem((size, size), bf16),
        vmem((size, size), bf16),
        vmem((n, n), bf16),
        vmem((n, n), bf16),
        vmem((2, channels, 2 * channels), f32),
        vmem((1, channels, 2 * channels), f32),
        vmem((chunks, 2 * channels, wide), bf16),
        vmem((channels, lanes), f32),
        vmem((1, channels), f32),
        vmem((planes, 1, channels), f32),
        vmem((1, channels), f32),
        vmem((1, channels), f32),
        vmem((1, channels), f32),
        vmem((2, 16, channels), f32),
        vmem((2, 8, channels), f32),
        vmem((planes, 16, channels), bf16),
        vmem((planes, 8, channels), bf16),
        vmem((planes, 16, channels), bf16),
        vmem((planes, 8, channels), bf16),
        vmem((16, channels), bf16),
        vmem((8, channels), bf16),
        sems((6 * chunks,)), sems((6, chunks)), sems((chunks,)), sems((chunks,)), sems((mine,)), sems((mine,)),
        sems((2, 3)), sems((2, 3)), sems((2, chunks)), sems((2,)), sems((5,)),
    ]
    in_any = pl.BlockSpec(memory_space=pl.ANY)
    shape = jax.ShapeDtypeStruct
    results = pl.pallas_call(
        functools.partial(kernel, devices),
        out_shape=(
            shape(pair.shape, bf16),
            shape(pair.shape, bf16),
            shape((planes, 16, channels), bf16),
            shape((planes, 8, channels), bf16),
            shape((1, channels), f32),
        ),
        in_specs=[in_any] * 8,
        out_specs=[in_any] * 5,
        scratch_shapes=scratch,
        compiler_params=pltpu.CompilerParams(collective_id=0, has_side_effects=True, vmem_limit_bytes=56 * 2**20),
        cost_estimate=pl.CostEstimate(flops=2 * 10**9, bytes_accessed=3 * 10**6, transcendentals=10**6),
        name="exchange",
    )(pair, grad_out, pad_mask, chain_ids, chain_bias.reshape(1, channels), w_in, w_gate, w_out)
    out = pl.pallas_call(
        finish,
        out_shape=(
            shape(pair.shape, bf16),
            shape(pair.shape, bf16),
            shape(w_in.shape, f32),
            shape(w_gate.shape, f32),
            shape(w_out.shape, f32),
            shape((1, channels), f32),
        ),
        in_specs=[in_any] * 5,
        out_specs=[in_any] * 6,
        scratch_shapes=[
            vmem((planes, 16, channels), bf16), vmem((planes, 8, channels), bf16), vmem(pair.shape, bf16), vmem(pair.shape, bf16),
            vmem(w_in.shape, f32), vmem(w_gate.shape, f32), vmem(w_out.shape, f32), vmem((1, channels), f32),
            sems((3 + 2 * chunks,)), sems((4 + 2 * chunks,)),
        ],
        compiler_params=pltpu.CompilerParams(vmem_limit_bytes=56 * 2**20),
        cost_estimate=pl.CostEstimate(flops=10**6, bytes_accessed=4 * 10**6, transcendentals=0),
        name="finish",
    )(*results)
    return (*out[:5], out[5].reshape(channels))


def solution(mesh):
    placed = (P(("dp", "dap"), None, None), P(("dp", "dap"), None, None), P("dp"), P("dp"), P(), P(), P(), P())
    return jax.shard_map(
        functools.partial(on_device, mesh.shape["dap"]),
        mesh=mesh,
        in_specs=placed,
        out_specs=(
            P(("dp", "dap"), None, None),
            P(("dp", "dap"), None, None),
            P("dp", None),
            P("dp", None),
            P("dp", None),
            P("dp"),
        ),
        check_vma=False,
    )
```

```python
import functools

import jax
import jax.numpy as jnp
from jax import lax
from jax.experimental import pallas as pl
from jax.experimental.pallas import tpu as pltpu
from jax.sharding import PartitionSpec as P

epsilon = 1e-05
f32 = jnp.float32
bf16 = jnp.bfloat16

CORES = 2
PAIR = 2
B, A, X, DX, DA, DB = range(6)
EARLY, LATE = range(2)


def nn(left, right):
    return jnp.dot(left, right, preferred_element_type=f32)


def nt(left, right):
    return lax.dot_general(left, right, (((1,), (1,)), ((), ())), preferred_element_type=f32)


def tn(left, right):
    return lax.dot_general(left, right, (((0,), (0,)), ((), ())), preferred_element_type=f32)


def sigmoid(values):
    return 0.5 * jnp.tanh(0.5 * values) + 0.5


def mean0(values):
    return jnp.mean(values, axis=0, keepdims=True)


def kernel(
    devices,
    pair_hbm, gout_hbm, pad_hbm, chain_hbm, bias_hbm, w_in_hbm, w_gate_hbm, w_out_hbm,
    update, gpair, sums_early, sums_late, chain_out,
    pair, gout, pad_v, chain_v, pad_s, chain_s, bias, w_in, w_gate, w_out, in_sem,
    s_snd, s_rcv, b_all, ch_a, ch_dx, db_part, db_snd, db_rcv, ch_db,
    z, rz, sig_a, lin_a, sig_b, lin_b, gate, gout_t, du, acc, xn, ds,
    bias_t, wt_in, wt_gate, wt_out, gather, scatter, order, order_t,
    g_early, g_late, both_v, chain_sum, chain_snd, chain_rcv, chain_own, chain_other,
    core_early, core_late, rs_early, rs_late, got_early, got_late, ag_early, ag_late,
    s_ssem, s_rsem, b_ssem, b_rsem, d_ssem, d_rsem, g_ssem, g_rsem, c_sem,
):
    rows, n, channels = pair.shape
    planes = devices // CORES
    chunks = rows // PAIR
    lanes = n // chunks
    mine = channels // planes
    part = planes * PAIR
    size = part * mine
    me = lax.axis_index("dap")
    plane = lax.div(me, CORES)
    core = lax.rem(me, CORES)
    other = plane * CORES + 1 - core

    side = 4 if planes == 32 else 2
    offsets = [(dz, dy, dx) for dz in range(side) for dy in range(side) for dx in range(2)]
    offsets.sort(key=lambda o: -(min(o[0], side - o[0]) + min(o[1], side - o[1]) + o[2]))
    at_z, at_y, at_x = lax.div(plane, 2 * side), lax.rem(lax.div(plane, 2), side), lax.rem(plane, 2)

    def plane_peer(k):
        dz, dy, dx = offsets[k - 1]
        to = (lax.rem(at_z + dz, side) * side + lax.rem(at_y + dy, side)) * 2 + lax.rem(at_x + dx, 2)
        return to, to * CORES + core

    barrier = pltpu.get_barrier_semaphore()
    greeted = [plane_peer(k)[1] for k in range(1, planes)] + [other]
    for device in greeted:
        pl.semaphore_signal(barrier, inc=1, device_id={"dap": device}, device_id_type=pl.DeviceIdType.MESH)

    loads = [
        pltpu.make_async_copy(src, dst, in_sem.at[i])
        for i, (src, dst) in enumerate((
            (pad_hbm, pad_v), (chain_hbm, chain_v), (pad_hbm, pad_s), (chain_hbm, chain_s), (bias_hbm, bias), (w_in_hbm, w_in),
            *((pair_hbm.at[pl.ds(p * PAIR, PAIR)], pair.at[pl.ds(p * PAIR, PAIR)]) for p in range(chunks)),
            (w_gate_hbm, w_gate), (w_out_hbm, w_out), (gout_hbm, gout),
        ))
    ]
    for load in loads:
        load.start()

    def loaded(count):
        for _ in range(count):
            loads.pop(0).wait()

    def remote(src, dst, ssem, rsem, device):
        pltpu.make_async_remote_copy(
            src_ref=src, dst_ref=dst, send_sem=ssem, recv_sem=rsem,
            device_id={"dap": device}, device_id_type=pl.DeviceIdType.MESH,
        ).start()

    def wait(ref, sem):
        pltpu.make_async_copy(ref, ref, sem).wait()

    def s_sent(step):
        wait(s_snd.at[0, 0, pl.ds(0, planes - 1)], s_ssem.at[step])

    def s_send(u, p):
        if u != B or p >= 2:
            s_sent(u * chunks + p - 2)
        for k in range(1, planes):
            to, device = plane_peer(k)
            remote(s_snd.at[u, p, to], s_rcv.at[u, p, plane], s_ssem.at[u * chunks + p], s_rsem.at[u, p], device)
        s_rcv[u, p, plane] = s_snd[u, p, plane]

    def s_wait(u, p):
        wait(s_rcv.at[u, p, pl.ds(0, planes - 1)], s_rsem.at[u, p])

    def to_channels(u, p):
        s_wait(u, p)
        return nn(gather[...], s_rcv[u, p].reshape(size, n)).astype(bf16)

    def to_rows(u, p, values):
        s_snd[u, p] = nn(scatter[...], values).astype(bf16).reshape(planes, PAIR * mine, n)
        s_send(u, p)

    def span(kt):
        return pl.ds(pl.multiple_of(kt * lanes, lanes), lanes)

    groups = channels // 8
    low = lax.broadcasted_iota(jnp.int32, (groups, 8, lanes), 1) < 4

    def swap(first, second):
        return (
            jnp.where(low, first, pltpu.roll(second, 4, 1)),
            jnp.where(low, pltpu.roll(first, 4, 1), second),
        )

    def put(u, p, kt, block):
        first, second = [block[:, h * lanes:(h + 1) * lanes].reshape(groups, 8, lanes) for h in range(PAIR)]
        even, odd = swap(first, second)
        s_snd[u, p, :, :, span(kt)] = jnp.stack([even, odd], axis=1).reshape(planes, 8, lanes).astype(bf16)

    def take(u, p, kt):
        block = s_rcv[u, p, :, :, span(kt)].astype(f32).reshape(groups, 2, 8, lanes)
        first, second = swap(block[:, 0], block[:, 1])
        return jnp.concatenate([first.reshape(channels, lanes), second.reshape(channels, lanes)], axis=1)

    def turned(ref, p, kt):
        return jnp.concatenate([ref[p * PAIR + h, span(kt), :].astype(f32).T for h in range(PAIR)], axis=1)

    def turn_back(ref, p, kt, block):
        for h in range(PAIR):
            ref[p * PAIR + h, span(kt), :] = block[:, h * lanes:(h + 1) * lanes].T.astype(bf16)

    def same_of(p, kt):
        ids = chain_v[span(kt)].reshape(1, lanes)
        return jnp.concatenate([(ids == chain_s[me * rows + p * PAIR + h]).astype(f32) for h in range(PAIR)], axis=1)

    def mask_of(p, kt):
        pad = pad_v[span(kt)].reshape(1, lanes)
        return jnp.concatenate([(pad * pad_s[me * rows + p * PAIR + h]).astype(f32) for h in range(PAIR)], axis=1)

    def project(u, p, kt, sig_ref, lin_ref, first):
        blk = p * chunks + kt
        both = nn(wt_in[first:first + 2 * channels, :], z[blk])
        sig, lin = sigmoid(both[:channels]), both[channels:]
        sig_ref[blk] = sig
        lin_ref[blk] = lin
        put(u, p, kt, sig * lin * mask_of(p, kt))

    def turn_in(first):
        wt_in[first:first + channels, :] = w_in[:, first:first + channels].astype(f32).T.astype(bf16)

    loaded(6)
    turn_in(2 * channels)
    turn_in(3 * channels)
    bias_t[...] = jnp.broadcast_to(bias[...], (channels, channels)).T

    def start_block(p, kt):
        blk = p * chunks + kt
        col = bias_t[:, 0:1]
        values = turned(pair, p, kt) + same_of(p, kt) * col
        center = values - mean0(values)
        inverse = lax.rsqrt(mean0(center * center) + epsilon)
        z[blk] = (center * inverse).astype(bf16)
        rz[blk] = inverse
        project(B, p, kt, sig_b, lin_b, 2 * channels)

    def start_chunk(p):
        loaded(1)

        @pl.loop(0, chunks)
        def _(kt):
            start_block(p, kt)

    def a_chunk(p):
        @pl.loop(0, chunks)
        def _(kt):
            project(A, p, kt, sig_a, lin_a, 0)

    def at_owner(i):
        return lax.rem(i, part) * mine + lax.div(i, part)

    def natural(i):
        row, own = lax.rem(i, PAIR), lax.rem(lax.div(i, PAIR), planes)
        p, at = lax.rem(lax.div(i, part), chunks), lax.div(i, part * chunks)
        return (own * CORES + at) * rows + p * PAIR + row

    def ones_at(down, along):
        return (down == along).astype(f32).astype(bf16)

    def down(k):
        return lax.broadcasted_iota(jnp.int32, (k, 1), 0)

    def along(k):
        return lax.broadcasted_iota(jnp.int32, (1, k), 1)

    def pass_on(p):
        b_all[:, core, p] = to_channels(B, p).reshape(mine, part, n)
        here = b_all.at[:, core, p]
        remote(here, here, b_ssem.at[p], b_rsem.at[p], other)

    def gates(p):
        @pl.loop(0, chunks)
        def _(kt):
            blk = p * chunks + kt
            g = sigmoid(nn(wt_gate[...], z[blk]))
            cot = turned(gout, p, kt)
            gate[blk] = g
            gout_t[blk] = cot
            grad_u = (cot * g).astype(bf16)
            du[blk] = grad_u
            acc[blk] = nn(w_out[...], grad_u)

    start_chunk(0)
    pl.semaphore_wait(barrier, len(greeted))
    s_send(B, 0)
    start_chunk(1)
    s_send(B, 1)
    start_chunk(2)
    turn_in(0)
    turn_in(channels)
    a_chunk(0)
    s_send(B, 2)
    a_chunk(1)
    scatter[...] = ones_at(down(size), at_owner(along(size)))
    gather[...] = ones_at(lax.rem(down(size), part) * mine + lax.div(down(size), part), along(size))
    pass_on(0)
    s_send(A, 0)
    a_chunk(2)
    order[...] = ones_at(down(n), natural(along(n)))
    order_t[...] = ones_at(natural(down(n)), along(n))
    pass_on(1)
    s_send(A, 1)
    loaded(3)
    wt_gate[...] = w_gate[...].astype(f32).T.astype(bf16)
    wt_out[...] = w_out[...].astype(f32).T.astype(bf16)
    gates(0)
    pass_on(2)
    s_send(A, 2)

    @pl.loop(0, chunks)
    def _(p):
        wait(b_all.at[:, 1 - core, p], b_rsem.at[p])

    def b_of(c):
        return b_all[c].reshape(n, n)

    @pl.loop(0, chunks)
    def _(p):
        ch_a[p] = to_channels(A, p).reshape(mine, part, n)
        got = jnp.concatenate([nt(ch_a[p, c], b_of(c)).astype(bf16) for c in range(mine)], axis=0)
        to_rows(X, p, nn(got, order_t[...]).astype(bf16))

    @pl.loop(1, chunks)
    def _(p):
        gates(p)

    g_early[...] = jnp.zeros_like(g_early)
    g_late[...] = jnp.zeros_like(g_late)
    chain_sum[...] = jnp.zeros_like(chain_sum)

    @pl.loop(0, chunks)
    def _(p):
        s_wait(X, p)

        @pl.loop(0, chunks)
        def _(kt):
            blk = p * chunks + kt
            values = take(X, p, kt)
            center = values - mean0(values)
            inverse = lax.rsqrt(mean0(center * center) + epsilon)
            normed = center * inverse
            xn[blk] = normed.astype(bf16)
            grad = acc[blk]
            grad = inverse * (grad - mean0(grad) - normed * mean0(grad * normed))
            put(DX, p, kt, grad)

        s_send(DX, p)

        @pl.loop(0, chunks)
        def _(kt):
            blk = p * chunks + kt
            lin = nn(wt_out[...], xn[blk])
            g = gate[blk]
            turn_back(update, p, kt, g * lin)
            grad_s = (gout_t[blk] * lin * g * (1.0 - g)).astype(bf16)
            ds[blk] = grad_s
            g_early[1, :, :channels] += nt(z[blk], grad_s)
            g_early[1, :, channels:] += nt(xn[blk], du[blk])

    @pl.loop(0, chunks)
    def _(p):
        ch_dx[p] = nn(to_channels(DX, p), order[...]).astype(bf16).reshape(mine, part, n)
        got = jnp.concatenate([nn(ch_dx[p, c], b_of(c)).astype(bf16) for c in range(mine)], axis=0)
        to_rows(DA, p, got)

    @pl.loop(0, mine)
    def _(c):
        left = jnp.concatenate([ch_dx[p, c] for p in range(chunks)], axis=0)
        right = jnp.concatenate([ch_a[p, c] for p in range(chunks)], axis=0)
        db_part[c] = tn(left, right).reshape(CORES, chunks * part, n)
        db_snd[c] = db_part[c, 1 - core].astype(bf16)
        remote(db_snd.at[c], db_rcv.at[c], d_ssem.at[c], d_rsem.at[c], other)

    @pl.loop(0, mine)
    def _(c):
        wait(db_rcv.at[c], d_rsem.at[c])
        total = (db_part[c, core] + db_rcv[c].astype(f32)).astype(bf16)
        for p in range(chunks):
            ch_db[p, c] = total[p * part:(p + 1) * part]

    @pl.loop(0, chunks)
    def _(p):
        to_rows(DB, p, ch_db[p].reshape(size, n))

    def grad_project(u, p, kt, sig_ref, lin_ref):
        blk = p * chunks + kt
        sig = sig_ref[blk]
        grad = take(u, p, kt) * mask_of(p, kt) * sig
        return jnp.concatenate([(grad * lin_ref[blk] * (1.0 - sig)).astype(bf16), grad.astype(bf16)], axis=0)

    @pl.loop(0, chunks)
    def _(p):
        s_wait(DA, p)

        @pl.loop(0, chunks)
        def _(kt):
            blk = p * chunks + kt
            both = grad_project(DA, p, kt, sig_a, lin_a)
            g_early[0] += nt(z[blk], both)
            acc[blk] = nn(w_in[:, :2 * channels], both) + nn(w_gate[...], ds[blk])

    grads = (g_early, g_late)
    cores = (core_early, core_late)
    rs_snd, rs_rcv = (rs_early, rs_late), (got_early, got_late)
    ag_snd, sums = (ag_early, ag_late), (sums_early, sums_late)
    others = pl.ds(0, planes - 1)

    def send_rows(src, dst, group, step):
        for k in range(1, planes):
            to, device = plane_peer(k)
            remote(src(to), dst.at[plane], g_ssem.at[group, step], g_rsem.at[group, step], device)

    def sum_planes(group):
        tiles = []
        for at in range(grads[group].shape[0]):
            halves = [grads[group][at, :, h * channels:(h + 1) * channels].reshape(groups, 8, channels) for h in range(2)]
            tiles.append(jnp.stack(swap(*halves), axis=1).reshape(planes, 8, channels))
        rs_snd[group][...] = jnp.concatenate(tiles, axis=1).astype(bf16)
        send_rows(lambda to: rs_snd[group].at[to], rs_rcv[group], group, 0)
        rs_rcv[group][plane] = rs_snd[group][plane]

    def sum_cores(group):
        wait(rs_rcv[group].at[others], g_rsem.at[group, 0])
        cores[group][0] = jnp.sum(rs_rcv[group][...].astype(f32), axis=0) * (1.0 / n)
        remote(cores[group].at[0], cores[group].at[1], g_ssem.at[group, 1], g_rsem.at[group, 1], other)

    def share(group):
        wait(cores[group].at[1], g_rsem.at[group, 1])
        ag_snd[group][...] = (cores[group][0] + cores[group][1]).astype(bf16)
        send_rows(lambda to: ag_snd[group], sums[group], group, 2)
        sums[group][plane] = ag_snd[group][...]

    def last_sums(p):
        s_wait(DB, p)

        @pl.loop(0, chunks)
        def _(kt):
            both = grad_project(DB, p, kt, sig_b, lin_b)
            both_v[kt] = both
            g_late[0] += nt(z[p * chunks + kt], both)

    def last_grads(p):
        @pl.loop(0, chunks)
        def _(kt):
            blk = p * chunks + kt
            grad = acc[blk] + nn(w_in[:, 2 * channels:], both_v[kt])
            normed = z[blk].astype(f32)
            grad = rz[blk] * (grad - mean0(grad) - normed * mean0(grad * normed))
            turn_back(gpair, p, kt, grad)
            grad = grad * same_of(p, kt)
            chain_sum[...] += grad[:, :lanes] + grad[:, lanes:]

    @pl.loop(0, chunks - 2)
    def _(p):
        last_sums(p)
        last_grads(p)

    s_sent(DB * chunks + chunks - 2)
    s_sent(DB * chunks + chunks - 1)
    sum_planes(EARLY)
    last_sums(chunks - 2)
    last_grads(chunks - 2)
    last_sums(chunks - 1)
    sum_planes(LATE)
    last_grads(chunks - 1)
    chain_snd[...] = jnp.sum(chain_sum[...].T, axis=0, keepdims=True)
    for k in range(1, planes):
        remote(chain_snd, chain_rcv.at[plane], c_sem.at[0], c_sem.at[1], plane_peer(k)[1])
    chain_rcv[plane] = chain_snd[...]
    sum_cores(EARLY)
    share(EARLY)
    sum_cores(LATE)
    wait(chain_rcv.at[others], c_sem.at[1])
    chain_own[...] = jnp.sum(chain_rcv[...], axis=0) * (1.0 / n)
    remote(chain_own, chain_other, c_sem.at[2], c_sem.at[3], other)
    share(LATE)
    wait(chain_other, c_sem.at[3])
    chain_out[...] = chain_own[...] + chain_other[...]

    @pl.loop(0, chunks)
    def _(p):
        wait(b_all.at[:, core, p], b_ssem.at[p])

    @pl.loop(0, mine)
    def _(c):
        wait(db_snd.at[c], d_ssem.at[c])

    for group in (EARLY, LATE):
        wait(rs_snd[group].at[others], g_ssem.at[group, 0])
        wait(cores[group].at[0], g_ssem.at[group, 1])
        wait(sums[group].at[others], g_ssem.at[group, 2])
        wait(sums[group].at[others], g_rsem.at[group, 2])

    wait(chain_rcv.at[others], c_sem.at[0])
    wait(chain_own, c_sem.at[2])


def finish(
    update_v, gpair_v, early, late, chain, update, gpair, gw_in, gw_gate, gw_out, gw_chain,
    in_v, gate_v, out_v, out_sem,
):
    channels = update.shape[2]
    groups = channels // 8
    stores = []

    def store(src, dst):
        stores.append(pltpu.make_async_copy(src, dst, out_sem.at[len(stores)]))
        stores[-1].start()

    store(update_v, update)
    store(gpair_v, gpair)
    store(chain, gw_chain)
    low = lax.broadcasted_iota(jnp.int32, (groups, 8, channels), 1) < 4

    def whole(sums, at):
        block = sums[...].astype(f32)[:, at * 8:(at + 1) * 8].reshape(groups, 2, 8, channels)
        even, odd = block[:, 0], block[:, 1]
        first = jnp.where(low, even, pltpu.roll(odd, 4, 1))
        second = jnp.where(low, pltpu.roll(even, 4, 1), odd)
        return first.reshape(channels, channels), second.reshape(channels, channels)

    for i, part in enumerate(whole(early, 0) + whole(late, 0)):
        in_v[:, i * channels:(i + 1) * channels] = part
    store(in_v, gw_in)
    gate_v[...], out_v[...] = whole(early, 1)
    store(gate_v, gw_gate)
    store(out_v, gw_out)
    for out in stores:
        out.wait()


def on_device(devices, pair, grad_out, pad_mask, chain_ids, chain_bias, w_in, w_gate, w_out):
    rows, n, channels = pair.shape
    planes = devices // CORES
    chunks = rows // PAIR
    lanes = n // chunks
    mine = channels // planes
    part = planes * PAIR
    size = part * mine
    blocks = chunks * chunks
    wide = PAIR * lanes
    vmem, sems = pltpu.VMEM, pltpu.SemaphoreType.DMA
    scratch = [
        vmem(pair.shape, bf16),
        vmem(pair.shape, bf16),
        vmem((n,), jnp.int32),
        vmem((n,), jnp.int32),
        pltpu.SMEM((n,), jnp.int32),
        pltpu.SMEM((n,), jnp.int32),
        vmem((1, channels), f32),
        vmem(w_in.shape, bf16),
        vmem(w_gate.shape, bf16),
        vmem(w_out.shape, bf16),
        sems((9 + chunks,)),
        vmem((6, chunks, planes, PAIR * mine, n), bf16),
        vmem((6, chunks, planes, PAIR * mine, n), bf16),
        vmem((mine, CORES, chunks, part, n), bf16),
        vmem((chunks, mine, part, n), bf16),
        vmem((chunks, mine, part, n), bf16),
        vmem((mine, CORES, chunks * part, n), f32),
        vmem((mine, chunks * part, n), bf16),
        vmem((mine, chunks * part, n), bf16),
        vmem((chunks, mine, part, n), bf16),
        vmem((blocks, channels, wide), bf16),
        vmem((blocks, 1, wide), f32),
        vmem((blocks, channels, wide), f32),
        vmem((blocks, channels, wide), f32),
        vmem((blocks, channels, wide), f32),
        vmem((blocks, channels, wide), f32),
        vmem((blocks, channels, wide), f32),
        vmem((blocks, channels, wide), f32),
        vmem((blocks, channels, wide), bf16),
        vmem((blocks, channels, wide), f32),
        vmem((blocks, channels, wide), bf16),
        vmem((blocks, channels, wide), bf16),
        vmem((channels, channels), f32),
        vmem((4 * channels, channels), bf16),
        vmem((channels, channels), bf16),
        vmem((channels, channels), bf16),
        vmem((size, size), bf16),
        vmem((size, size), bf16),
        vmem((n, n), bf16),
        vmem((n, n), bf16),
        vmem((2, channels, 2 * channels), f32),
        vmem((1, channels, 2 * channels), f32),
        vmem((chunks, 2 * channels, wide), bf16),
        vmem((channels, lanes), f32),
        vmem((1, channels), f32),
        vmem((planes, 1, channels), f32),
        vmem((1, channels), f32),
        vmem((1, channels), f32),
        vmem((2, 16, channels), f32),
        vmem((2, 8, channels), f32),
        vmem((planes, 16, channels), bf16),
        vmem((planes, 8, channels), bf16),
        vmem((planes, 16, channels), bf16),
        vmem((planes, 8, channels), bf16),
        vmem((16, channels), bf16),
        vmem((8, channels), bf16),
        sems((6 * chunks,)), sems((6, chunks)), sems((chunks,)), sems((chunks,)), sems((mine,)), sems((mine,)),
        sems((2, 3)), sems((2, 3)), sems((4,)),
    ]
    in_any = pl.BlockSpec(memory_space=pl.ANY)
    in_vmem = pl.BlockSpec(memory_space=pltpu.VMEM)
    shape = jax.ShapeDtypeStruct
    results = pl.pallas_call(
        functools.partial(kernel, devices),
        out_shape=(
            vmem(pair.shape, bf16),
            vmem(pair.shape, bf16),
            vmem((planes, 16, channels), bf16),
            vmem((planes, 8, channels), bf16),
            vmem((1, channels), f32),
        ),
        in_specs=[in_any] * 8,
        out_specs=[in_vmem] * 5,
        scratch_shapes=scratch,
        compiler_params=pltpu.CompilerParams(collective_id=0, has_side_effects=True, vmem_limit_bytes=56 * 2**20),
        cost_estimate=pl.CostEstimate(flops=2 * 10**9, bytes_accessed=3 * 10**6, transcendentals=10**6),
        name="exchange",
    )(pair, grad_out, pad_mask, chain_ids, chain_bias.reshape(1, channels), w_in, w_gate, w_out)
    out = pl.pallas_call(
        finish,
        out_shape=(
            shape(pair.shape, bf16),
            shape(pair.shape, bf16),
            shape(w_in.shape, f32),
            shape(w_gate.shape, f32),
            shape(w_out.shape, f32),
            shape((1, channels), f32),
        ),
        in_specs=[in_vmem] * 5,
        out_specs=[in_any] * 6,
        scratch_shapes=[vmem(w_in.shape, f32), vmem(w_gate.shape, f32), vmem(w_out.shape, f32), sems((6,))],
        compiler_params=pltpu.CompilerParams(vmem_limit_bytes=16 * 2**20),
        cost_estimate=pl.CostEstimate(flops=10**6, bytes_accessed=4 * 10**6, transcendentals=0),
        name="finish",
    )(*results)
    return (*out[:5], out[5].reshape(channels))


def solution(mesh):
    placed = (P(("dp", "dap"), None, None), P(("dp", "dap"), None, None), P("dp"), P("dp"), P(), P(), P(), P())
    return jax.shard_map(
        functools.partial(on_device, mesh.shape["dap"]),
        mesh=mesh,
        in_specs=placed,
        out_specs=(
            P(("dp", "dap"), None, None),
            P(("dp", "dap"), None, None),
            P("dp", None),
            P("dp", None),
            P("dp", None),
            P("dp"),
        ),
        check_vma=False,
    )
```

```python
import functools

import jax
import jax.numpy as jnp
from jax import lax
from jax.experimental import pallas as pl
from jax.experimental.pallas import tpu as pltpu
from jax.sharding import PartitionSpec as P

epsilon = 1e-05
f32 = jnp.float32
bf16 = jnp.bfloat16

CORES = 2
PAIR = 2
B, A, X, DX, DA, DB = range(6)
EARLY, LATE = range(2)


def nn(left, right):
    return jnp.dot(left, right, preferred_element_type=f32)


def nt(left, right):
    return lax.dot_general(left, right, (((1,), (1,)), ((), ())), preferred_element_type=f32)


def tn(left, right):
    return lax.dot_general(left, right, (((0,), (0,)), ((), ())), preferred_element_type=f32)


def sigmoid(values):
    return 0.5 * jnp.tanh(0.5 * values) + 0.5


def mean0(values):
    return jnp.mean(values, axis=0, keepdims=True)


def kernel(
    devices,
    pair_hbm, gout_hbm, pad_hbm, chain_hbm, bias_hbm, w_in_hbm, w_gate_hbm, w_out_hbm,
    update, gpair, sums_early, sums_late, chain_out,
    pair, gout, pad_v, chain_v, pad_s, chain_s, bias, w_in, w_gate, w_out, in_sem,
    s_snd, s_rcv, b_all, ch_a, ch_dx, db_part, db_snd, db_rcv, ch_db,
    z, rz, sig_a, lin_a, sig_b, lin_b, gate, gout_t, du, acc, xn, ds,
    bias_t, wt_in, wt_gate, wt_out, gather, scatter, order, order_t,
    g_early, g_late, both_v, chain_sum, chain_snd, chain_rcv, chain_own, chain_other,
    core_early, rs_early, rs_late, got_early, got_late, ag_early, ag_late,
    s_ssem, s_rsem, b_ssem, b_rsem, d_ssem, d_rsem, g_ssem, g_rsem, c_sem,
):
    rows, n, channels = pair.shape
    planes = devices // CORES
    chunks = rows // PAIR
    lanes = n // chunks
    mine = channels // planes
    part = planes * PAIR
    size = part * mine
    me = lax.axis_index("dap")
    plane = lax.div(me, CORES)
    core = lax.rem(me, CORES)
    other = plane * CORES + 1 - core

    side = 4 if planes == 32 else 2
    offsets = [(dz, dy, dx) for dz in range(side) for dy in range(side) for dx in range(2)]
    offsets.sort(key=lambda o: -(min(o[0], side - o[0]) + min(o[1], side - o[1]) + o[2]))
    at_z, at_y, at_x = lax.div(plane, 2 * side), lax.rem(lax.div(plane, 2), side), lax.rem(plane, 2)

    def plane_peer(k):
        dz, dy, dx = offsets[k - 1]
        to = (lax.rem(at_z + dz, side) * side + lax.rem(at_y + dy, side)) * 2 + lax.rem(at_x + dx, 2)
        return to, to * CORES + core

    barrier = pltpu.get_barrier_semaphore()
    greeted = [plane_peer(k)[1] for k in range(1, planes)] + [plane_peer(k)[1] + 1 - 2 * core for k in range(1, planes)] + [other]
    for device in greeted:
        pl.semaphore_signal(barrier, inc=1, device_id={"dap": device}, device_id_type=pl.DeviceIdType.MESH)

    loads = [
        pltpu.make_async_copy(src, dst, in_sem.at[i])
        for i, (src, dst) in enumerate((
            (pad_hbm, pad_v), (chain_hbm, chain_v), (pad_hbm, pad_s), (chain_hbm, chain_s), (bias_hbm, bias), (w_in_hbm, w_in),
            *((pair_hbm.at[pl.ds(p * PAIR, PAIR)], pair.at[pl.ds(p * PAIR, PAIR)]) for p in range(chunks)),
            (w_gate_hbm, w_gate), (w_out_hbm, w_out), (gout_hbm, gout),
        ))
    ]
    for load in loads:
        load.start()

    def loaded(count):
        for _ in range(count):
            loads.pop(0).wait()

    def remote(src, dst, ssem, rsem, device):
        pltpu.make_async_remote_copy(
            src_ref=src, dst_ref=dst, send_sem=ssem, recv_sem=rsem,
            device_id={"dap": device}, device_id_type=pl.DeviceIdType.MESH,
        ).start()

    def wait(ref, sem):
        pltpu.make_async_copy(ref, ref, sem).wait()

    def s_sent(step):
        wait(s_snd.at[0, 0, pl.ds(0, planes - 1)], s_ssem.at[step])

    def s_send(u, p):
        for k in range(1, planes):
            to, device = plane_peer(k)
            remote(s_snd.at[u, p, to], s_rcv.at[u, p, plane], s_ssem.at[u * chunks + p], s_rsem.at[u, p], device)
        s_rcv[u, p, plane] = s_snd[u, p, plane]

    def s_wait(u, p):
        wait(s_rcv.at[u, p, pl.ds(0, planes - 1)], s_rsem.at[u, p])

    def to_channels(u, p):
        s_wait(u, p)
        return nn(gather[...], s_rcv[u, p].reshape(size, n)).astype(bf16)

    def to_rows(u, p, values):
        s_snd[u, p] = nn(scatter[...], values).astype(bf16).reshape(planes, PAIR * mine, n)
        s_send(u, p)

    def span(kt):
        return pl.ds(pl.multiple_of(kt * lanes, lanes), lanes)

    groups = channels // 8
    low = lax.broadcasted_iota(jnp.int32, (groups, 8, lanes), 1) < 4

    def swap(first, second):
        return (
            jnp.where(low, first, pltpu.roll(second, 4, 1)),
            jnp.where(low, pltpu.roll(first, 4, 1), second),
        )

    def put(u, p, kt, block):
        first, second = [block[:, h * lanes:(h + 1) * lanes].reshape(groups, 8, lanes) for h in range(PAIR)]
        even, odd = swap(first, second)
        s_snd[u, p, :, :, span(kt)] = jnp.stack([even, odd], axis=1).reshape(planes, 8, lanes).astype(bf16)

    def take(u, p, kt):
        block = s_rcv[u, p, :, :, span(kt)].astype(f32).reshape(groups, 2, 8, lanes)
        first, second = swap(block[:, 0], block[:, 1])
        return jnp.concatenate([first.reshape(channels, lanes), second.reshape(channels, lanes)], axis=1)

    def turned(ref, p, kt):
        return jnp.concatenate([ref[p * PAIR + h, span(kt), :].astype(f32).T for h in range(PAIR)], axis=1)

    def turn_back(ref, p, kt, block):
        for h in range(PAIR):
            ref[p * PAIR + h, span(kt), :] = block[:, h * lanes:(h + 1) * lanes].T.astype(bf16)

    def same_of(p, kt):
        ids = chain_v[span(kt)].reshape(1, lanes)
        return jnp.concatenate([(ids == chain_s[me * rows + p * PAIR + h]).astype(f32) for h in range(PAIR)], axis=1)

    def mask_of(p, kt):
        pad = pad_v[span(kt)].reshape(1, lanes)
        return jnp.concatenate([(pad * pad_s[me * rows + p * PAIR + h]).astype(f32) for h in range(PAIR)], axis=1)

    def project(u, p, kt, sig_ref, lin_ref, first):
        blk = p * chunks + kt
        both = nn(wt_in[first:first + 2 * channels, :], z[blk])
        sig, lin = sigmoid(both[:channels]), both[channels:]
        sig_ref[blk] = sig
        lin_ref[blk] = lin
        put(u, p, kt, sig * lin * mask_of(p, kt))

    def turn_in(first):
        wt_in[first:first + channels, :] = w_in[:, first:first + channels].astype(f32).T.astype(bf16)

    loaded(6)
    turn_in(2 * channels)
    turn_in(3 * channels)
    bias_t[...] = jnp.broadcast_to(bias[...], (channels, channels)).T

    def start_block(p, kt):
        blk = p * chunks + kt
        col = bias_t[:, 0:1]
        values = turned(pair, p, kt) + same_of(p, kt) * col
        center = values - mean0(values)
        inverse = lax.rsqrt(mean0(center * center) + epsilon)
        z[blk] = (center * inverse).astype(bf16)
        rz[blk] = inverse
        project(B, p, kt, sig_b, lin_b, 2 * channels)

    def start_chunk(p):
        loaded(1)

        @pl.loop(0, chunks)
        def _(kt):
            start_block(p, kt)

    def a_chunk(p):
        @pl.loop(0, chunks)
        def _(kt):
            project(A, p, kt, sig_a, lin_a, 0)

    def at_owner(i):
        return lax.rem(i, part) * mine + lax.div(i, part)

    def natural(i):
        row, own = lax.rem(i, PAIR), lax.rem(lax.div(i, PAIR), planes)
        p, at = lax.rem(lax.div(i, part), chunks), lax.div(i, part * chunks)
        return (own * CORES + at) * rows + p * PAIR + row

    def ones_at(down, along):
        return (down == along).astype(f32).astype(bf16)

    def down(k):
        return lax.broadcasted_iota(jnp.int32, (k, 1), 0)

    def along(k):
        return lax.broadcasted_iota(jnp.int32, (1, k), 1)

    def pass_on(p):
        b_all[:, core, p] = to_channels(B, p).reshape(mine, part, n)
        here = b_all.at[:, core, p]
        remote(here, here, b_ssem.at[p], b_rsem.at[p], other)

    def gates(p):
        @pl.loop(0, chunks)
        def _(kt):
            blk = p * chunks + kt
            g = sigmoid(nn(wt_gate[...], z[blk]))
            cot = turned(gout, p, kt)
            gate[blk] = g
            gout_t[blk] = cot
            grad_u = (cot * g).astype(bf16)
            du[blk] = grad_u
            acc[blk] = nn(w_out[...], grad_u)

    start_chunk(0)
    pl.semaphore_wait(barrier, len(greeted))
    s_send(B, 0)
    start_chunk(1)
    s_send(B, 1)
    start_chunk(2)
    turn_in(0)
    turn_in(channels)
    a_chunk(0)
    s_send(B, 2)
    a_chunk(1)
    scatter[...] = ones_at(down(size), at_owner(along(size)))
    gather[...] = ones_at(lax.rem(down(size), part) * mine + lax.div(down(size), part), along(size))
    pass_on(0)
    s_send(A, 0)
    a_chunk(2)
    order[...] = ones_at(down(n), natural(along(n)))
    order_t[...] = ones_at(natural(down(n)), along(n))
    pass_on(1)
    s_send(A, 1)
    loaded(3)
    wt_gate[...] = w_gate[...].astype(f32).T.astype(bf16)
    wt_out[...] = w_out[...].astype(f32).T.astype(bf16)
    gates(0)
    pass_on(2)
    s_send(A, 2)

    @pl.loop(0, chunks)
    def _(p):
        wait(b_all.at[:, 1 - core, p], b_rsem.at[p])

    def b_of(c):
        return b_all[c].reshape(n, n)

    @pl.loop(0, chunks)
    def _(p):
        ch_a[p] = to_channels(A, p).reshape(mine, part, n)
        got = jnp.concatenate([nt(ch_a[p, c], b_of(c)).astype(bf16) for c in range(mine)], axis=0)
        to_rows(X, p, nn(got, order_t[...]).astype(bf16))

    @pl.loop(1, chunks)
    def _(p):
        gates(p)

    g_early[...] = jnp.zeros_like(g_early)
    g_late[...] = jnp.zeros_like(g_late)
    chain_sum[...] = jnp.zeros_like(chain_sum)

    @pl.loop(0, chunks)
    def _(p):
        s_wait(X, p)

        @pl.loop(0, chunks)
        def _(kt):
            blk = p * chunks + kt
            values = take(X, p, kt)
            center = values - mean0(values)
            inverse = lax.rsqrt(mean0(center * center) + epsilon)
            normed = center * inverse
            xn[blk] = normed.astype(bf16)
            grad = acc[blk]
            grad = inverse * (grad - mean0(grad) - normed * mean0(grad * normed))
            put(DX, p, kt, grad)

        s_send(DX, p)

        @pl.loop(0, chunks)
        def _(kt):
            blk = p * chunks + kt
            lin = nn(wt_out[...], xn[blk])
            g = gate[blk]
            turn_back(update, p, kt, g * lin)
            grad_s = (gout_t[blk] * lin * g * (1.0 - g)).astype(bf16)
            ds[blk] = grad_s
            g_early[1, :, :channels] += nt(z[blk], grad_s)
            g_early[1, :, channels:] += nt(xn[blk], du[blk])

    @pl.loop(0, chunks)
    def _(p):
        ch_dx[p] = nn(to_channels(DX, p), order[...]).astype(bf16).reshape(mine, part, n)
        got = jnp.concatenate([nn(ch_dx[p, c], b_of(c)).astype(bf16) for c in range(mine)], axis=0)
        to_rows(DA, p, got)

    @pl.loop(0, mine)
    def _(c):
        left = jnp.concatenate([ch_dx[p, c] for p in range(chunks)], axis=0)
        right = jnp.concatenate([ch_a[p, c] for p in range(chunks)], axis=0)
        db_part[c] = tn(left, right).reshape(CORES, chunks * part, n)
        db_snd[c] = db_part[c, 1 - core].astype(bf16)
        remote(db_snd.at[c], db_rcv.at[c], d_ssem.at[c], d_rsem.at[c], other)

    @pl.loop(0, mine)
    def _(c):
        wait(db_rcv.at[c], d_rsem.at[c])
        total = (db_part[c, core] + db_rcv[c].astype(f32)).astype(bf16)
        for p in range(chunks):
            ch_db[p, c] = total[p * part:(p + 1) * part]

    @pl.loop(0, chunks)
    def _(p):
        to_rows(DB, p, ch_db[p].reshape(size, n))

    def grad_project(u, p, kt, sig_ref, lin_ref):
        blk = p * chunks + kt
        sig = sig_ref[blk]
        grad = take(u, p, kt) * mask_of(p, kt) * sig
        return jnp.concatenate([(grad * lin_ref[blk] * (1.0 - sig)).astype(bf16), grad.astype(bf16)], axis=0)

    @pl.loop(0, chunks)
    def _(p):
        s_wait(DA, p)

        @pl.loop(0, chunks)
        def _(kt):
            blk = p * chunks + kt
            both = grad_project(DA, p, kt, sig_a, lin_a)
            g_early[0] += nt(z[blk], both)
            acc[blk] = nn(w_in[:, :2 * channels], both) + nn(w_gate[...], ds[blk])

    grads = (g_early, g_late)
    rs_snd, rs_rcv = (rs_early, rs_late), (got_early, got_late)
    ag_snd, sums = (ag_early, ag_late), (sums_early, sums_late)
    others = pl.ds(0, planes - 1)

    def send_rows(src, dst, group, step):
        for k in range(1, planes):
            to, device = plane_peer(k)
            remote(src(to), dst.at[plane], g_ssem.at[group, step], g_rsem.at[group, step], device)

    def sum_planes(group):
        tiles = []
        for at in range(grads[group].shape[0]):
            halves = [grads[group][at, :, h * channels:(h + 1) * channels].reshape(groups, 8, channels) for h in range(2)]
            tiles.append(jnp.stack(swap(*halves), axis=1).reshape(planes, 8, channels))
        rs_snd[group][...] = jnp.concatenate(tiles, axis=1).astype(bf16)
        if group == EARLY:
            send_rows(lambda to: rs_snd[group].at[to], rs_rcv[group], group, 0)
            rs_rcv[group][plane] = rs_snd[group][plane]
            return
        for k in range(1, planes):
            to, device = plane_peer(k)
            for target in (device, device + 1 - 2 * core):
                remote(rs_snd[group].at[to], rs_rcv[group].at[me], g_ssem.at[group, 0], g_rsem.at[group, 0], target)
        remote(rs_snd[group].at[plane], rs_rcv[group].at[me], g_ssem.at[group, 0], g_rsem.at[group, 0], other)
        rs_rcv[group][me] = rs_snd[group][plane]

    def sum_cores():
        wait(got_early.at[others], g_rsem.at[EARLY, 0])
        core_early[0] = jnp.sum(got_early[...].astype(f32), axis=0) * (1.0 / n)
        remote(core_early.at[0], core_early.at[1], g_ssem.at[EARLY, 1], g_rsem.at[EARLY, 1], other)

    def share(group, rows):
        ag_snd[group][...] = rows.astype(bf16)
        send_rows(lambda to: ag_snd[group], sums[group], group, 2)
        sums[group][plane] = ag_snd[group][...]

    def share_early():
        wait(core_early.at[1], g_rsem.at[EARLY, 1])
        share(EARLY, core_early[0] + core_early[1])

    every_other = pl.ds(0, devices - 1)

    def share_late():
        wait(got_late.at[every_other], g_rsem.at[LATE, 0])
        share(LATE, jnp.sum(got_late[...].astype(f32), axis=0) * (1.0 / n))

    def last_sums(p):
        s_wait(DB, p)

        @pl.loop(0, chunks)
        def _(kt):
            both = grad_project(DB, p, kt, sig_b, lin_b)
            both_v[kt] = both
            g_late[0] += nt(z[p * chunks + kt], both)

    def last_grads(p):
        @pl.loop(0, chunks)
        def _(kt):
            blk = p * chunks + kt
            grad = acc[blk] + nn(w_in[:, 2 * channels:], both_v[kt])
            normed = z[blk].astype(f32)
            grad = rz[blk] * (grad - mean0(grad) - normed * mean0(grad * normed))
            turn_back(gpair, p, kt, grad)
            grad = grad * same_of(p, kt)
            chain_sum[...] += grad[:, :lanes] + grad[:, lanes:]

    @pl.loop(0, chunks - 2)
    def _(p):
        last_sums(p)
        last_grads(p)

    sum_planes(EARLY)
    last_sums(chunks - 2)
    last_grads(chunks - 2)
    last_sums(chunks - 1)
    sum_planes(LATE)
    last_grads(chunks - 1)
    chain_snd[...] = jnp.sum(chain_sum[...].T, axis=0, keepdims=True)
    for k in range(1, planes):
        remote(chain_snd, chain_rcv.at[plane], c_sem.at[0], c_sem.at[1], plane_peer(k)[1])
    chain_rcv[plane] = chain_snd[...]
    sum_cores()
    share_early()
    share_late()
    wait(chain_rcv.at[others], c_sem.at[1])
    chain_own[...] = jnp.sum(chain_rcv[...], axis=0) * (1.0 / n)
    remote(chain_own, chain_other, c_sem.at[2], c_sem.at[3], other)
    wait(chain_other, c_sem.at[3])
    chain_out[...] = chain_own[...] + chain_other[...]

    @pl.loop(0, 6 * chunks)
    def _(i):
        s_sent(i)

    @pl.loop(0, chunks)
    def _(p):
        wait(b_all.at[:, core, p], b_ssem.at[p])

    @pl.loop(0, mine)
    def _(c):
        wait(db_snd.at[c], d_ssem.at[c])

    for group in (EARLY, LATE):
        wait(sums[group].at[others], g_ssem.at[group, 2])
        wait(sums[group].at[others], g_rsem.at[group, 2])

    wait(rs_early.at[others], g_ssem.at[EARLY, 0])
    wait(got_late.at[every_other], g_ssem.at[LATE, 0])
    wait(core_early.at[0], g_ssem.at[EARLY, 1])
    wait(chain_rcv.at[others], c_sem.at[0])
    wait(chain_own, c_sem.at[2])


def finish(
    update_v, gpair_v, early, late, chain, update, gpair, gw_in, gw_gate, gw_out, gw_chain,
    in_v, gate_v, out_v, out_sem,
):
    channels = update.shape[2]
    groups = channels // 8
    stores = []

    def store(src, dst):
        stores.append(pltpu.make_async_copy(src, dst, out_sem.at[len(stores)]))
        stores[-1].start()

    store(update_v, update)
    store(gpair_v, gpair)
    store(chain, gw_chain)
    low = lax.broadcasted_iota(jnp.int32, (groups, 8, channels), 1) < 4

    def whole(sums, at):
        block = sums[...].astype(f32)[:, at * 8:(at + 1) * 8].reshape(groups, 2, 8, channels)
        even, odd = block[:, 0], block[:, 1]
        first = jnp.where(low, even, pltpu.roll(odd, 4, 1))
        second = jnp.where(low, pltpu.roll(even, 4, 1), odd)
        return first.reshape(channels, channels), second.reshape(channels, channels)

    for i, part in enumerate(whole(early, 0) + whole(late, 0)):
        in_v[:, i * channels:(i + 1) * channels] = part
    store(in_v, gw_in)
    gate_v[...], out_v[...] = whole(early, 1)
    store(gate_v, gw_gate)
    store(out_v, gw_out)
    for out in stores:
        out.wait()


def on_device(devices, pair, grad_out, pad_mask, chain_ids, chain_bias, w_in, w_gate, w_out):
    rows, n, channels = pair.shape
    planes = devices // CORES
    chunks = rows // PAIR
    lanes = n // chunks
    mine = channels // planes
    part = planes * PAIR
    size = part * mine
    blocks = chunks * chunks
    wide = PAIR * lanes
    vmem, sems = pltpu.VMEM, pltpu.SemaphoreType.DMA
    scratch = [
        vmem(pair.shape, bf16),
        vmem(pair.shape, bf16),
        vmem((n,), jnp.int32),
        vmem((n,), jnp.int32),
        pltpu.SMEM((n,), jnp.int32),
        pltpu.SMEM((n,), jnp.int32),
        vmem((1, channels), f32),
        vmem(w_in.shape, bf16),
        vmem(w_gate.shape, bf16),
        vmem(w_out.shape, bf16),
        sems((9 + chunks,)),
        vmem((6, chunks, planes, PAIR * mine, n), bf16),
        vmem((6, chunks, planes, PAIR * mine, n), bf16),
        vmem((mine, CORES, chunks, part, n), bf16),
        vmem((chunks, mine, part, n), bf16),
        vmem((chunks, mine, part, n), bf16),
        vmem((mine, CORES, chunks * part, n), f32),
        vmem((mine, chunks * part, n), bf16),
        vmem((mine, chunks * part, n), bf16),
        vmem((chunks, mine, part, n), bf16),
        vmem((blocks, channels, wide), bf16),
        vmem((blocks, 1, wide), f32),
        vmem((blocks, channels, wide), f32),
        vmem((blocks, channels, wide), f32),
        vmem((blocks, channels, wide), f32),
        vmem((blocks, channels, wide), f32),
        vmem((blocks, channels, wide), f32),
        vmem((blocks, channels, wide), f32),
        vmem((blocks, channels, wide), bf16),
        vmem((blocks, channels, wide), f32),
        vmem((blocks, channels, wide), bf16),
        vmem((blocks, channels, wide), bf16),
        vmem((channels, channels), f32),
        vmem((4 * channels, channels), bf16),
        vmem((channels, channels), bf16),
        vmem((channels, channels), bf16),
        vmem((size, size), bf16),
        vmem((size, size), bf16),
        vmem((n, n), bf16),
        vmem((n, n), bf16),
        vmem((2, channels, 2 * channels), f32),
        vmem((1, channels, 2 * channels), f32),
        vmem((chunks, 2 * channels, wide), bf16),
        vmem((channels, lanes), f32),
        vmem((1, channels), f32),
        vmem((planes, 1, channels), f32),
        vmem((1, channels), f32),
        vmem((1, channels), f32),
        vmem((2, 16, channels), f32),
        vmem((planes, 16, channels), bf16),
        vmem((planes, 8, channels), bf16),
        vmem((planes, 16, channels), bf16),
        vmem((devices, 8, channels), bf16),
        vmem((16, channels), bf16),
        vmem((8, channels), bf16),
        sems((6 * chunks,)), sems((6, chunks)), sems((chunks,)), sems((chunks,)), sems((mine,)), sems((mine,)),
        sems((2, 3)), sems((2, 3)), sems((4,)),
    ]
    in_any = pl.BlockSpec(memory_space=pl.ANY)
    in_vmem = pl.BlockSpec(memory_space=pltpu.VMEM)
    shape = jax.ShapeDtypeStruct
    results = pl.pallas_call(
        functools.partial(kernel, devices),
        out_shape=(
            vmem(pair.shape, bf16),
            vmem(pair.shape, bf16),
            vmem((planes, 16, channels), bf16),
            vmem((planes, 8, channels), bf16),
            vmem((1, channels), f32),
        ),
        in_specs=[in_any] * 8,
        out_specs=[in_vmem] * 5,
        scratch_shapes=scratch,
        compiler_params=pltpu.CompilerParams(collective_id=0, has_side_effects=True, vmem_limit_bytes=56 * 2**20),
        cost_estimate=pl.CostEstimate(flops=2 * 10**9, bytes_accessed=3 * 10**6, transcendentals=10**6),
        name="exchange",
    )(pair, grad_out, pad_mask, chain_ids, chain_bias.reshape(1, channels), w_in, w_gate, w_out)
    out = pl.pallas_call(
        finish,
        out_shape=(
            shape(pair.shape, bf16),
            shape(pair.shape, bf16),
            shape(w_in.shape, f32),
            shape(w_gate.shape, f32),
            shape(w_out.shape, f32),
            shape((1, channels), f32),
        ),
        in_specs=[in_vmem] * 5,
        out_specs=[in_any] * 6,
        scratch_shapes=[vmem(w_in.shape, f32), vmem(w_gate.shape, f32), vmem(w_out.shape, f32), sems((6,))],
        compiler_params=pltpu.CompilerParams(vmem_limit_bytes=16 * 2**20),
        cost_estimate=pl.CostEstimate(flops=10**6, bytes_accessed=4 * 10**6, transcendentals=0),
        name="finish",
    )(*results)
    return (*out[:5], out[5].reshape(channels))


def solution(mesh):
    placed = (P(("dp", "dap"), None, None), P(("dp", "dap"), None, None), P("dp"), P("dp"), P(), P(), P(), P())
    return jax.shard_map(
        functools.partial(on_device, mesh.shape["dap"]),
        mesh=mesh,
        in_specs=placed,
        out_specs=(
            P(("dp", "dap"), None, None),
            P(("dp", "dap"), None, None),
            P("dp", None),
            P("dp", None),
            P("dp", None),
            P("dp"),
        ),
        check_vma=False,
    )
```

```python
import functools

import jax
import jax.numpy as jnp
from jax import lax
from jax.experimental import pallas as pl
from jax.experimental.pallas import tpu as pltpu
from jax.sharding import PartitionSpec as P

epsilon = 1e-05
f32 = jnp.float32
bf16 = jnp.bfloat16

CORES = 2
PAIR = 2
B, A, X, DX, DA, DB = range(6)
EARLY, LATE = range(2)


def nn(left, right):
    return jnp.dot(left, right, preferred_element_type=f32)


def nt(left, right):
    return lax.dot_general(left, right, (((1,), (1,)), ((), ())), preferred_element_type=f32)


def tn(left, right):
    return lax.dot_general(left, right, (((0,), (0,)), ((), ())), preferred_element_type=f32)


def sigmoid(values):
    return 0.5 * jnp.tanh(0.5 * values) + 0.5


def mean0(values):
    return jnp.mean(values, axis=0, keepdims=True)


def kernel(
    devices,
    pair_hbm, gout_hbm, pad_hbm, chain_hbm, bias_hbm, w_in_hbm, w_gate_hbm, w_out_hbm,
    update, gpair, sums_early, sums_late, chain_out,
    pair, gout, pad_v, chain_v, pad_s, chain_s, bias, w_in, w_gate, w_out, in_sem,
    s_snd, s_rcv, b_all, ch_a, ch_dx, db_part, db_snd, db_rcv, ch_db,
    z, rz, sig_a, lin_a, sig_b, lin_b, gate, gout_t, du, acc, xn, ds,
    bias_t, wt_in, wt_gate, wt_out, gather, scatter, order, order_t,
    g_early, g_late, both_v, chain_sum, chain_snd, chain_rcv, chain_own, chain_other,
    core_early, rs_early, rs_late, got_early, got_late, ag_early, ag_late,
    s_ssem, s_rsem, b_ssem, b_rsem, d_ssem, d_rsem, g_ssem, g_rsem, c_sem,
):
    rows, n, channels = pair.shape
    planes = devices // CORES
    chunks = rows // PAIR
    lanes = n // chunks
    mine = channels // planes
    part = planes * PAIR
    size = part * mine
    me = lax.axis_index("dap")
    plane = lax.div(me, CORES)
    core = lax.rem(me, CORES)
    other = plane * CORES + 1 - core

    side = 4 if planes == 32 else 2
    offsets = [(dz, dy, dx) for dz in range(side) for dy in range(side) for dx in range(2)]
    offsets.sort(key=lambda o: -(min(o[0], side - o[0]) + min(o[1], side - o[1]) + o[2]))
    at_z, at_y, at_x = lax.div(plane, 2 * side), lax.rem(lax.div(plane, 2), side), lax.rem(plane, 2)

    def plane_peer(k):
        dz, dy, dx = offsets[k - 1]
        to = (lax.rem(at_z + dz, side) * side + lax.rem(at_y + dy, side)) * 2 + lax.rem(at_x + dx, 2)
        return to, to * CORES + core

    barrier = pltpu.get_barrier_semaphore()
    greeted = [plane_peer(k)[1] for k in range(1, planes)] + [plane_peer(k)[1] + 1 - 2 * core for k in range(1, planes)] + [other]
    for device in greeted:
        pl.semaphore_signal(barrier, inc=1, device_id={"dap": device}, device_id_type=pl.DeviceIdType.MESH)

    loads = [
        pltpu.make_async_copy(src, dst, in_sem.at[i])
        for i, (src, dst) in enumerate((
            (pad_hbm, pad_v), (chain_hbm, chain_v), (pad_hbm, pad_s), (chain_hbm, chain_s), (bias_hbm, bias), (w_in_hbm, w_in),
            *((pair_hbm.at[pl.ds(p * PAIR, PAIR)], pair.at[pl.ds(p * PAIR, PAIR)]) for p in range(chunks)),
            (w_gate_hbm, w_gate), (w_out_hbm, w_out), (gout_hbm, gout),
        ))
    ]
    for load in loads:
        load.start()

    def loaded(count):
        for _ in range(count):
            loads.pop(0).wait()

    def remote(src, dst, ssem, rsem, device):
        pltpu.make_async_remote_copy(
            src_ref=src, dst_ref=dst, send_sem=ssem, recv_sem=rsem,
            device_id={"dap": device}, device_id_type=pl.DeviceIdType.MESH,
        ).start()

    def wait(ref, sem):
        pltpu.make_async_copy(ref, ref, sem).wait()

    def s_sent(step):
        wait(s_snd.at[0, 0, pl.ds(0, planes - 1)], s_ssem.at[step])

    def s_send(u, p):
        for k in range(1, planes):
            to, device = plane_peer(k)
            remote(s_snd.at[u, p, to], s_rcv.at[u, p, plane], s_ssem.at[u * chunks + p], s_rsem.at[u, p], device)
        s_rcv[u, p, plane] = s_snd[u, p, plane]

    def s_wait(u, p):
        wait(s_rcv.at[u, p, pl.ds(0, planes - 1)], s_rsem.at[u, p])

    def to_channels(u, p):
        s_wait(u, p)
        return nn(gather[...], s_rcv[u, p].reshape(size, n)).astype(bf16)

    def to_rows(u, p, values):
        s_snd[u, p] = nn(scatter[...], values).astype(bf16).reshape(planes, PAIR * mine, n)
        s_send(u, p)

    def span(kt):
        return pl.ds(pl.multiple_of(kt * lanes, lanes), lanes)

    groups = channels // 8
    low = lax.broadcasted_iota(jnp.int32, (groups, 8, lanes), 1) < 4

    def swap(first, second):
        return (
            jnp.where(low, first, pltpu.roll(second, 4, 1)),
            jnp.where(low, pltpu.roll(first, 4, 1), second),
        )

    def put(u, p, kt, block):
        first, second = [block[:, h * lanes:(h + 1) * lanes].reshape(groups, 8, lanes) for h in range(PAIR)]
        even, odd = swap(first, second)
        s_snd[u, p, :, :, span(kt)] = jnp.stack([even, odd], axis=1).reshape(planes, 8, lanes).astype(bf16)

    def take(u, p, kt):
        block = s_rcv[u, p, :, :, span(kt)].astype(f32).reshape(groups, 2, 8, lanes)
        first, second = swap(block[:, 0], block[:, 1])
        return jnp.concatenate([first.reshape(channels, lanes), second.reshape(channels, lanes)], axis=1)

    def turned(ref, p, kt):
        return jnp.concatenate([ref[p * PAIR + h, span(kt), :].astype(f32).T for h in range(PAIR)], axis=1)

    def turn_back(ref, p, kt, block):
        for h in range(PAIR):
            ref[p * PAIR + h, span(kt), :] = block[:, h * lanes:(h + 1) * lanes].T.astype(bf16)

    def same_of(p, kt):
        ids = chain_v[span(kt)].reshape(1, lanes)
        return jnp.concatenate([(ids == chain_s[me * rows + p * PAIR + h]).astype(f32) for h in range(PAIR)], axis=1)

    def mask_of(p, kt):
        pad = pad_v[span(kt)].reshape(1, lanes)
        return jnp.concatenate([(pad * pad_s[me * rows + p * PAIR + h]).astype(f32) for h in range(PAIR)], axis=1)

    def project(u, p, kt, sig_ref, lin_ref, first):
        blk = p * chunks + kt
        both = nn(wt_in[first:first + 2 * channels, :], z[blk])
        sig, lin = sigmoid(both[:channels]), both[channels:]
        masked = sig * mask_of(p, kt)
        value = masked * lin
        sig_ref[blk] = masked
        lin_ref[blk] = value * (1.0 - sig)
        put(u, p, kt, value)

    def turn_in(first):
        wt_in[first:first + channels, :] = w_in[:, first:first + channels].astype(f32).T.astype(bf16)

    loaded(6)
    turn_in(2 * channels)
    turn_in(3 * channels)
    bias_t[...] = jnp.broadcast_to(bias[...], (channels, channels)).T

    def start_block(p, kt):
        blk = p * chunks + kt
        col = bias_t[:, 0:1]
        values = turned(pair, p, kt) + same_of(p, kt) * col
        center = values - mean0(values)
        inverse = lax.rsqrt(mean0(center * center) + epsilon)
        z[blk] = (center * inverse).astype(bf16)
        rz[blk] = inverse
        project(B, p, kt, sig_b, lin_b, 2 * channels)

    def start_chunk(p):
        loaded(1)

        @pl.loop(0, chunks)
        def _(kt):
            start_block(p, kt)

    def a_chunk(p):
        @pl.loop(0, chunks)
        def _(kt):
            project(A, p, kt, sig_a, lin_a, 0)

    def at_owner(i):
        return lax.rem(i, part) * mine + lax.div(i, part)

    def natural(i):
        row, own = lax.rem(i, PAIR), lax.rem(lax.div(i, PAIR), planes)
        p, at = lax.rem(lax.div(i, part), chunks), lax.div(i, part * chunks)
        return (own * CORES + at) * rows + p * PAIR + row

    def ones_at(down, along):
        return (down == along).astype(f32).astype(bf16)

    def down(k):
        return lax.broadcasted_iota(jnp.int32, (k, 1), 0)

    def along(k):
        return lax.broadcasted_iota(jnp.int32, (1, k), 1)

    def pass_on(p):
        b_all[:, core, p] = to_channels(B, p).reshape(mine, part, n)
        here = b_all.at[:, core, p]
        remote(here, here, b_ssem.at[p], b_rsem.at[p], other)

    def gates(p):
        @pl.loop(0, chunks)
        def _(kt):
            blk = p * chunks + kt
            g = sigmoid(nn(wt_gate[...], z[blk]))
            cot = turned(gout, p, kt)
            gate[blk] = g
            gout_t[blk] = cot
            grad_u = (cot * g).astype(bf16)
            du[blk] = grad_u
            acc[blk] = nn(w_out[...], grad_u)

    start_chunk(0)
    pl.semaphore_wait(barrier, len(greeted))
    s_send(B, 0)
    start_chunk(1)
    s_send(B, 1)
    start_chunk(2)
    turn_in(0)
    turn_in(channels)
    a_chunk(0)
    s_send(B, 2)
    a_chunk(1)
    scatter[...] = ones_at(down(size), at_owner(along(size)))
    gather[...] = ones_at(lax.rem(down(size), part) * mine + lax.div(down(size), part), along(size))
    pass_on(0)
    s_send(A, 0)
    a_chunk(2)
    order[...] = ones_at(down(n), natural(along(n)))
    order_t[...] = ones_at(natural(down(n)), along(n))
    pass_on(1)
    s_send(A, 1)
    loaded(3)
    wt_gate[...] = w_gate[...].astype(f32).T.astype(bf16)
    wt_out[...] = w_out[...].astype(f32).T.astype(bf16)
    gates(0)
    pass_on(2)
    s_send(A, 2)

    @pl.loop(0, chunks)
    def _(p):
        wait(b_all.at[:, 1 - core, p], b_rsem.at[p])

    def b_of(c):
        return b_all[c].reshape(n, n)

    @pl.loop(0, chunks)
    def _(p):
        ch_a[p] = to_channels(A, p).reshape(mine, part, n)
        got = jnp.concatenate([nt(ch_a[p, c], b_of(c)).astype(bf16) for c in range(mine)], axis=0)
        to_rows(X, p, nn(got, order_t[...]).astype(bf16))

    @pl.loop(1, chunks)
    def _(p):
        gates(p)

    g_early[...] = jnp.zeros_like(g_early)
    g_late[...] = jnp.zeros_like(g_late)
    chain_sum[...] = jnp.zeros_like(chain_sum)

    @pl.loop(0, chunks)
    def _(p):
        s_wait(X, p)

        @pl.loop(0, chunks)
        def _(kt):
            blk = p * chunks + kt
            values = take(X, p, kt)
            center = values - mean0(values)
            inverse = lax.rsqrt(mean0(center * center) + epsilon)
            normed = center * inverse
            xn[blk] = normed.astype(bf16)
            grad = acc[blk]
            grad = inverse * (grad - mean0(grad) - normed * mean0(grad * normed))
            put(DX, p, kt, grad)

        s_send(DX, p)

        @pl.loop(0, chunks)
        def _(kt):
            blk = p * chunks + kt
            lin = nn(wt_out[...], xn[blk])
            g = gate[blk]
            turn_back(update, p, kt, g * lin)
            grad_s = (gout_t[blk] * lin * g * (1.0 - g)).astype(bf16)
            ds[blk] = grad_s
            g_early[1, :, :channels] += nt(z[blk], grad_s)
            g_early[1, :, channels:] += nt(xn[blk], du[blk])

    @pl.loop(0, chunks)
    def _(p):
        ch_dx[p] = nn(to_channels(DX, p), order[...]).astype(bf16).reshape(mine, part, n)
        got = jnp.concatenate([nn(ch_dx[p, c], b_of(c)).astype(bf16) for c in range(mine)], axis=0)
        to_rows(DA, p, got)

    @pl.loop(0, mine)
    def _(c):
        left = jnp.concatenate([ch_dx[p, c] for p in range(chunks)], axis=0)
        right = jnp.concatenate([ch_a[p, c] for p in range(chunks)], axis=0)
        db_part[c] = tn(left, right).reshape(CORES, chunks * part, n)
        db_snd[c] = db_part[c, 1 - core].astype(bf16)
        remote(db_snd.at[c], db_rcv.at[c], d_ssem.at[c], d_rsem.at[c], other)

    @pl.loop(0, mine)
    def _(c):
        wait(db_rcv.at[c], d_rsem.at[c])
        total = (db_part[c, core] + db_rcv[c].astype(f32)).astype(bf16)
        for p in range(chunks):
            ch_db[p, c] = total[p * part:(p + 1) * part]

    @pl.loop(0, chunks)
    def _(p):
        to_rows(DB, p, ch_db[p].reshape(size, n))

    def grad_project(u, p, kt, sig_ref, lin_ref):
        blk = p * chunks + kt
        grad = take(u, p, kt)
        return jnp.concatenate([(grad * lin_ref[blk]).astype(bf16), (grad * sig_ref[blk]).astype(bf16)], axis=0)

    @pl.loop(0, chunks)
    def _(p):
        s_wait(DA, p)

        @pl.loop(0, chunks)
        def _(kt):
            blk = p * chunks + kt
            both = grad_project(DA, p, kt, sig_a, lin_a)
            g_early[0] += nt(z[blk], both)
            acc[blk] = nn(w_in[:, :2 * channels], both) + nn(w_gate[...], ds[blk])

    grads = (g_early, g_late)
    rs_snd, rs_rcv = (rs_early, rs_late), (got_early, got_late)
    ag_snd, sums = (ag_early, ag_late), (sums_early, sums_late)
    others = pl.ds(0, planes - 1)

    def send_rows(src, dst, group, step):
        for k in range(1, planes):
            to, device = plane_peer(k)
            remote(src(to), dst.at[plane], g_ssem.at[group, step], g_rsem.at[group, step], device)

    def sum_planes(group):
        tiles = []
        for at in range(grads[group].shape[0]):
            halves = [grads[group][at, :, h * channels:(h + 1) * channels].reshape(groups, 8, channels) for h in range(2)]
            tiles.append(jnp.stack(swap(*halves), axis=1).reshape(planes, 8, channels))
        rs_snd[group][...] = jnp.concatenate(tiles, axis=1).astype(bf16)
        if group == EARLY:
            send_rows(lambda to: rs_snd[group].at[to], rs_rcv[group], group, 0)
            rs_rcv[group][plane] = rs_snd[group][plane]
            return
        for k in range(1, planes):
            to, device = plane_peer(k)
            for target in (device, device + 1 - 2 * core):
                remote(rs_snd[group].at[to], rs_rcv[group].at[me], g_ssem.at[group, 0], g_rsem.at[group, 0], target)
        remote(rs_snd[group].at[plane], rs_rcv[group].at[me], g_ssem.at[group, 0], g_rsem.at[group, 0], other)
        rs_rcv[group][me] = rs_snd[group][plane]

    def sum_cores():
        wait(got_early.at[others], g_rsem.at[EARLY, 0])
        core_early[0] = jnp.sum(got_early[...].astype(f32), axis=0) * (1.0 / n)
        remote(core_early.at[0], core_early.at[1], g_ssem.at[EARLY, 1], g_rsem.at[EARLY, 1], other)

    def share(group, rows):
        ag_snd[group][...] = rows.astype(bf16)
        send_rows(lambda to: ag_snd[group], sums[group], group, 2)
        sums[group][plane] = ag_snd[group][...]

    def share_early():
        wait(core_early.at[1], g_rsem.at[EARLY, 1])
        share(EARLY, core_early[0] + core_early[1])

    every_other = pl.ds(0, devices - 1)

    def share_late():
        wait(got_late.at[every_other], g_rsem.at[LATE, 0])
        share(LATE, jnp.sum(got_late[...].astype(f32), axis=0) * (1.0 / n))

    def last_sums(p):
        s_wait(DB, p)

        @pl.loop(0, chunks)
        def _(kt):
            both = grad_project(DB, p, kt, sig_b, lin_b)
            both_v[kt] = both
            g_late[0] += nt(z[p * chunks + kt], both)

    def last_grads(p):
        @pl.loop(0, chunks)
        def _(kt):
            blk = p * chunks + kt
            grad = acc[blk] + nn(w_in[:, 2 * channels:], both_v[kt])
            normed = z[blk].astype(f32)
            grad = rz[blk] * (grad - mean0(grad) - normed * mean0(grad * normed))
            turn_back(gpair, p, kt, grad)
            grad = grad * same_of(p, kt)
            chain_sum[...] += grad[:, :lanes] + grad[:, lanes:]

    @pl.loop(0, chunks - 2)
    def _(p):
        last_sums(p)
        last_grads(p)

    sum_planes(EARLY)
    last_sums(chunks - 2)
    last_grads(chunks - 2)
    last_sums(chunks - 1)
    sum_planes(LATE)
    last_grads(chunks - 1)
    chain_snd[...] = jnp.sum(chain_sum[...].T, axis=0, keepdims=True)
    for k in range(1, planes):
        remote(chain_snd, chain_rcv.at[plane], c_sem.at[0], c_sem.at[1], plane_peer(k)[1])
    chain_rcv[plane] = chain_snd[...]
    sum_cores()
    share_early()
    share_late()
    wait(chain_rcv.at[others], c_sem.at[1])
    chain_own[...] = jnp.sum(chain_rcv[...], axis=0) * (1.0 / n)
    remote(chain_own, chain_other, c_sem.at[2], c_sem.at[3], other)
    wait(chain_other, c_sem.at[3])
    chain_out[...] = chain_own[...] + chain_other[...]

    @pl.loop(0, 6 * chunks)
    def _(i):
        s_sent(i)

    @pl.loop(0, chunks)
    def _(p):
        wait(b_all.at[:, core, p], b_ssem.at[p])

    @pl.loop(0, mine)
    def _(c):
        wait(db_snd.at[c], d_ssem.at[c])

    for group in (EARLY, LATE):
        wait(sums[group].at[others], g_ssem.at[group, 2])
        wait(sums[group].at[others], g_rsem.at[group, 2])

    wait(rs_early.at[others], g_ssem.at[EARLY, 0])
    wait(got_late.at[every_other], g_ssem.at[LATE, 0])
    wait(core_early.at[0], g_ssem.at[EARLY, 1])
    wait(chain_rcv.at[others], c_sem.at[0])
    wait(chain_own, c_sem.at[2])


def finish(
    update_v, gpair_v, early, late, chain, update, gpair, gw_in, gw_gate, gw_out, gw_chain,
    in_v, gate_v, out_v, out_sem,
):
    channels = update.shape[2]
    groups = channels // 8
    stores = []

    def store(src, dst):
        stores.append(pltpu.make_async_copy(src, dst, out_sem.at[len(stores)]))
        stores[-1].start()

    store(update_v, update)
    store(gpair_v, gpair)
    store(chain, gw_chain)
    low = lax.broadcasted_iota(jnp.int32, (groups, 8, channels), 1) < 4

    def whole(sums, at):
        block = sums[...].astype(f32)[:, at * 8:(at + 1) * 8].reshape(groups, 2, 8, channels)
        even, odd = block[:, 0], block[:, 1]
        first = jnp.where(low, even, pltpu.roll(odd, 4, 1))
        second = jnp.where(low, pltpu.roll(even, 4, 1), odd)
        return first.reshape(channels, channels), second.reshape(channels, channels)

    for i, part in enumerate(whole(early, 0) + whole(late, 0)):
        in_v[:, i * channels:(i + 1) * channels] = part
    store(in_v, gw_in)
    gate_v[...], out_v[...] = whole(early, 1)
    store(gate_v, gw_gate)
    store(out_v, gw_out)
    for out in stores:
        out.wait()


def on_device(devices, pair, grad_out, pad_mask, chain_ids, chain_bias, w_in, w_gate, w_out):
    rows, n, channels = pair.shape
    planes = devices // CORES
    chunks = rows // PAIR
    lanes = n // chunks
    mine = channels // planes
    part = planes * PAIR
    size = part * mine
    blocks = chunks * chunks
    wide = PAIR * lanes
    vmem, sems = pltpu.VMEM, pltpu.SemaphoreType.DMA
    scratch = [
        vmem(pair.shape, bf16),
        vmem(pair.shape, bf16),
        vmem((n,), jnp.int32),
        vmem((n,), jnp.int32),
        pltpu.SMEM((n,), jnp.int32),
        pltpu.SMEM((n,), jnp.int32),
        vmem((1, channels), f32),
        vmem(w_in.shape, bf16),
        vmem(w_gate.shape, bf16),
        vmem(w_out.shape, bf16),
        sems((9 + chunks,)),
        vmem((6, chunks, planes, PAIR * mine, n), bf16),
        vmem((6, chunks, planes, PAIR * mine, n), bf16),
        vmem((mine, CORES, chunks, part, n), bf16),
        vmem((chunks, mine, part, n), bf16),
        vmem((chunks, mine, part, n), bf16),
        vmem((mine, CORES, chunks * part, n), f32),
        vmem((mine, chunks * part, n), bf16),
        vmem((mine, chunks * part, n), bf16),
        vmem((chunks, mine, part, n), bf16),
        vmem((blocks, channels, wide), bf16),
        vmem((blocks, 1, wide), f32),
        vmem((blocks, channels, wide), f32),
        vmem((blocks, channels, wide), f32),
        vmem((blocks, channels, wide), f32),
        vmem((blocks, channels, wide), f32),
        vmem((blocks, channels, wide), f32),
        vmem((blocks, channels, wide), f32),
        vmem((blocks, channels, wide), bf16),
        vmem((blocks, channels, wide), f32),
        vmem((blocks, channels, wide), bf16),
        vmem((blocks, channels, wide), bf16),
        vmem((channels, channels), f32),
        vmem((4 * channels, channels), bf16),
        vmem((channels, channels), bf16),
        vmem((channels, channels), bf16),
        vmem((size, size), bf16),
        vmem((size, size), bf16),
        vmem((n, n), bf16),
        vmem((n, n), bf16),
        vmem((2, channels, 2 * channels), f32),
        vmem((1, channels, 2 * channels), f32),
        vmem((chunks, 2 * channels, wide), bf16),
        vmem((channels, lanes), f32),
        vmem((1, channels), f32),
        vmem((planes, 1, channels), f32),
        vmem((1, channels), f32),
        vmem((1, channels), f32),
        vmem((2, 16, channels), f32),
        vmem((planes, 16, channels), bf16),
        vmem((planes, 8, channels), bf16),
        vmem((planes, 16, channels), bf16),
        vmem((devices, 8, channels), bf16),
        vmem((16, channels), bf16),
        vmem((8, channels), bf16),
        sems((6 * chunks,)), sems((6, chunks)), sems((chunks,)), sems((chunks,)), sems((mine,)), sems((mine,)),
        sems((2, 3)), sems((2, 3)), sems((4,)),
    ]
    in_any = pl.BlockSpec(memory_space=pl.ANY)
    in_vmem = pl.BlockSpec(memory_space=pltpu.VMEM)
    shape = jax.ShapeDtypeStruct
    results = pl.pallas_call(
        functools.partial(kernel, devices),
        out_shape=(
            vmem(pair.shape, bf16),
            vmem(pair.shape, bf16),
            vmem((planes, 16, channels), bf16),
            vmem((planes, 8, channels), bf16),
            vmem((1, channels), f32),
        ),
        in_specs=[in_any] * 8,
        out_specs=[in_vmem] * 5,
        scratch_shapes=scratch,
        compiler_params=pltpu.CompilerParams(collective_id=0, has_side_effects=True, vmem_limit_bytes=56 * 2**20),
        cost_estimate=pl.CostEstimate(flops=2 * 10**9, bytes_accessed=3 * 10**6, transcendentals=10**6),
        name="exchange",
    )(pair, grad_out, pad_mask, chain_ids, chain_bias.reshape(1, channels), w_in, w_gate, w_out)
    out = pl.pallas_call(
        finish,
        out_shape=(
            shape(pair.shape, bf16),
            shape(pair.shape, bf16),
            shape(w_in.shape, f32),
            shape(w_gate.shape, f32),
            shape(w_out.shape, f32),
            shape((1, channels), f32),
        ),
        in_specs=[in_vmem] * 5,
        out_specs=[in_any] * 6,
        scratch_shapes=[vmem(w_in.shape, f32), vmem(w_gate.shape, f32), vmem(w_out.shape, f32), sems((6,))],
        compiler_params=pltpu.CompilerParams(vmem_limit_bytes=16 * 2**20),
        cost_estimate=pl.CostEstimate(flops=10**6, bytes_accessed=4 * 10**6, transcendentals=0),
        name="finish",
    )(*results)
    return (*out[:5], out[5].reshape(channels))


def solution(mesh):
    placed = (P(("dp", "dap"), None, None), P(("dp", "dap"), None, None), P("dp"), P("dp"), P(), P(), P(), P())
    return jax.shard_map(
        functools.partial(on_device, mesh.shape["dap"]),
        mesh=mesh,
        in_specs=placed,
        out_specs=(
            P(("dp", "dap"), None, None),
            P(("dp", "dap"), None, None),
            P("dp", None),
            P("dp", None),
            P("dp", None),
            P("dp"),
        ),
        check_vma=False,
    )
```
